128 devices in a mesh: year: 4 (over z_lo, core), tile: 32 (over x, z_hi, y).
Axes of the slice: x: 4, y: 4, z: 4 (z_hi: 2, z_lo: 2; z = z_hi * 2 + z_lo), core: 2. Of those that a mesh axis runs over, the one named last changes fastest.
Arguments:
- station_tile: int32 [131072, 1], P(('year', 'tile')), may hold values from 0 to 31; in each aligned block of 1024 rows (0 to 1023, 1024 to 2047, ...) at most 96 rows name the same one
- station_cell: int32 [131072], P(('year', 'tile')), may hold values from 0 to 262143
- station_value: float32 [131072], P(('year', 'tile')), may hold values from -6 to 6
- class_ids: int32 [128, 8192], P(None, 'tile'), may hold values from 0 to 15
- coeff_table: float32 [3, 16], replicated, may hold values from 0.2 to 2
- lag_blocks: float32 [5, 128, 128], replicated, may hold values from -0.5 to 0.5
Outputs:
- filtered: float32 [32, 128, 8192], P('year', None, 'tile')
The draws below stay inside these ranges and needn't reach their ends.
Inputs may be any that keep to these rules, and one draw needn't show every extreme that they name: `station_tile`: in the rows of one device no tile is named by more than 96 rows, a bound that some block reaches.
All inputs are finite; a program needn't handle non-finite values.
Results may differ from the reference program's by a relative error of at most 0.00013.
Values sent between devices are 32-bit elements; how exact they have to be, the bound alone decides.
A program may use at most 192 MiB of HBM per device.

```python
import math
import jax
import jax.numpy as jnp
import numpy as np
from jax import lax

DAY_DEV = 8
LAT = 128
LON_DEV = 256
STN_DEV = 1024
NCLASS = 16
CAP = 96
DAYS = 32
LON = 8192
STATIONS = 131072
N_TILE = 32


def plant(drawn, stream_key, low, largest):
    place = [jax.random.randint(jax.random.fold_in(stream_key, axis), (), 0, length) for axis, length in enumerate(drawn.shape)]
    widest = drawn.shape.index(max(drawn.shape))
    next_to = place[:widest] + [(place[widest] + 1) % drawn.shape[widest]] + place[widest + 1:]
    return drawn.at[tuple(place)].set(low).at[tuple(next_to)].set(largest)


def steps_of(own_key, extent, cuts, smallest, largest):
    level = 1.0
    for axis_at, blocks in cuts:
        steps = jax.random.uniform(jax.random.fold_in(jax.random.fold_in(own_key, 6), axis_at), (blocks,), jnp.float32, smallest / len(cuts), largest / len(cuts))
        level = level * jnp.repeat(jnp.exp(steps), extent[axis_at] // blocks).reshape((-1,) + (1,) * (len(extent) - 1 - axis_at))
    return level


def assign_block(rng, own, number, rows, count, top, bound, skew):
    sequence = jax.random.permutation(rng, count)
    crowded, common = portions_of(count, rows * top, bound, skew, True), portions_of(count, rows * top, bound, skew, False)
    places = jnp.arange(count)

    def named(tallies, rotation):
        used = int((tallies > 0).sum())
        fixed = max(1, used // 4)
        passed = fixed + (places - fixed + rotation * (used - fixed)) % max(1, count - fixed)
        return jnp.zeros((count,), jnp.int32).at[sequence[jnp.where(places < fixed, places, passed)]].set(jnp.asarray(tallies, jnp.int32))

    tallies = jnp.where(number % 4 == 0, named(crowded, number // 4), named(common, number - number // 4 - 1))
    mixed = jax.random.permutation(jax.random.fold_in(own, 3), count)
    giver, taker = mixed[0:count // 2 * 2:2], mixed[1:count // 2 * 2:2]
    room = jnp.minimum(tallies[giver] - 1, bound - tallies[taker]) // 2
    room = jnp.where((giver == sequence[0]) | (taker == sequence[0]) | (tallies[taker] == 0), 0, jnp.maximum(room, 0))
    passed = jax.random.randint(jax.random.fold_in(own, 4), (count // 2,), 0, 1 << 20) % (room + 1)
    tallies = tallies.at[giver].add(-passed).at[taker].add(passed)
    items = jnp.searchsorted(jnp.cumsum(tallies), jnp.arange(rows * top), side="right").astype(jnp.int32)
    table = items.reshape(top, rows).T
    table = table[jax.random.permutation(jax.random.fold_in(own, 1), rows)]
    rotation = jax.random.randint(jax.random.fold_in(own, 2), (rows, 1), 0, top)
    return jnp.take_along_axis(table, (jnp.arange(top)[None, :] + rotation) % top, axis=1)


def portions_of(count, total, reach, skew, full):
    weights = [(1 << 20) // math.isqrt(rank ** skew) + 1 for rank in range(1, count + 1)]
    largest = reach if full else min(reach, max(-(-total // count), total * weights[0] // sum(weights)))
    least = 1 if total - largest >= count - 1 else 0
    counts, surplus = [largest] + [least] * (count - 1), total - largest - least * (count - 1)
    while surplus > 0:
        free = [i for i in range(1, count) if counts[i] < largest] or [i for i in range(1, count) if counts[i] < reach]
        mass, budget = sum([weights[i] for i in free]), surplus
        for i in free:
            more = min(reach - counts[i], max(1, budget * weights[i] // mass), surplus)
            counts[i] = counts[i] + more
            surplus = surplus - more
    return np.array(counts)


def bell_draw(stream_key, shape, deviation, limit, cuts=(), held_as=jnp.bfloat16):
    drawn = jax.random.normal(stream_key, shape, jnp.float32) * deviation
    if len(cuts) > 0:
        drawn = steps_of(stream_key, shape, cuts, -0.22, 0.18) * drawn
    return jnp.clip(drawn, min=-limit, max=limit).astype(held_as)


def setup_inputs(seed: int = 0) -> dict:
    keys = jax.random.split(jax.random.key(seed), 7)
    station_tile_keys = jax.random.split(jax.random.fold_in(keys[0], 1), STATIONS // STN_DEV)
    station_tile_turns = jax.random.permutation(jax.random.fold_in(keys[0], 3), STATIONS // STN_DEV)
    station_tile = jax.vmap(lambda own, number: assign_block(jax.random.fold_in(keys[0], 2), own, number, STN_DEV, N_TILE, 1, CAP, 2))(station_tile_keys, station_tile_turns).reshape((STATIONS, 1))
    station_cell = plant(jax.random.randint(keys[1], (STATIONS,), 0, DAY_DEV * LAT * LON_DEV), jax.random.fold_in(keys[1], 1), 0, (DAY_DEV * LAT * LON_DEV) - 1).astype(jnp.int32)
    station_value = bell_draw(keys[2], (STATIONS,), 1.0, 6.0, ((0, 128),), jnp.float32)
    class_ids = plant(jax.random.randint(keys[3], (LAT, LON), 0, NCLASS), jax.random.fold_in(keys[3], 1), 0, NCLASS - 1).astype(jnp.int32)
    coeff_table = jnp.clip(jnp.exp(jax.random.uniform(keys[4], (3, NCLASS), jnp.float32, math.log(0.2), math.log(2.0))), 0.2, 2.0)
    lag_blocks = bell_draw(keys[5], (5, LAT, LAT), LAT ** -0.5, 0.5, (), jnp.float32)
    return {"station_tile": station_tile, "station_cell": station_cell, "station_value": station_value, "class_ids": class_ids, "coeff_table": coeff_table, "lag_blocks": lag_blocks}


def apply_op(field, kappa, hzon, hmer):
    east = jnp.roll(field, -1, axis=2)
    west = jnp.roll(field, 1, axis=2)
    zeros_row = jnp.zeros_like(field[:, :1, :])
    north = jnp.concatenate([field[:, 1:, :], zeros_row], axis=1)
    south = jnp.concatenate([zeros_row, field[:, :-1, :]], axis=1)
    return kappa * field + hzon * (2.0 * field - east - west) + hmer * (2.0 * field - north - south)


def reference(station_tile, station_cell, station_value, class_ids, coeff_table, lag_blocks):
    plane = LAT * LON_DEV
    index = jnp.arange(STATIONS, dtype=jnp.int32)
    segment = index // (STN_DEV * N_TILE)
    day = segment * DAY_DEV + station_cell // plane
    row = (station_cell // LON_DEV) % LAT
    lon = station_tile[:, 0] * LON_DEV + station_cell % LON_DEV
    flat = (day * LAT + row) * LON + lon
    residual_field = jnp.zeros((DAYS * LAT * LON,), jnp.float32).at[flat].add(station_value)
    residual_field = residual_field.reshape(DAYS, LAT, LON)
    kappa = coeff_table[0][class_ids]
    hzon = coeff_table[1][class_ids]
    hmer = coeff_table[2][class_ids]
    spatial = apply_op(apply_op(residual_field, kappa, hzon, hmer), kappa, hzon, hmer)
    filtered = jnp.zeros_like(spatial)
    for k in range(5):
        moved = jnp.roll(spatial, -(k - 2), axis=0)
        filtered = filtered + jnp.einsum("ij,djk->dik", lag_blocks[k], moved, precision=lax.Precision.HIGHEST)
    return filtered
```

```python
import jax
import jax.numpy as jnp
from jax import lax
from jax.experimental import pallas as pl
from jax.experimental.pallas import tpu as pltpu
from jax.sharding import PartitionSpec as P

DAY_DEV = 8
LAT = 128
LON_DEV = 256
CAP = 96
LANES = 128
NTILE = 32
NYEAR = 4
NCLASS = 16
LAGS = 5
HALO = 2
DAYS_EXT = DAY_DEV + 2 * HALO
PAD = 8
F32 = jnp.float32
BF16 = jnp.bfloat16


def dot_nt(a, b):
    return lax.dot_general(a, b, (((1,), (1,)), ((), ())), preferred_element_type=F32)


def split2(x):
    hi = x.astype(BF16).astype(F32)
    return hi, x - hi


def hot(mask):
    return jnp.where(mask, 1.0, 0.0).astype(BF16)


def bucket(tile_ref, cell_ref, value_ref, pieces_ref, slots_ref, send_ref):
    tile = tile_ref[...]
    cell = cell_ref[...]
    hi, mid = split2(value_ref[...])
    day = jnp.right_shift(cell, 15).astype(F32)
    row = jnp.bitwise_and(jnp.right_shift(cell, 8), 127).astype(F32)
    col = jnp.bitwise_and(cell, 255).astype(F32)
    of_tile = lax.broadcasted_iota(jnp.int32, (NTILE, LANES), 0)
    masks = [tile[b : b + 1, :] == of_tile for b in range(8)]
    ones = jnp.concatenate([hot(m) for m in masks], axis=0)
    source = lax.broadcasted_iota(jnp.int32, (LANES, 2 * LANES), 0)
    target = lax.broadcasted_iota(jnp.int32, (LANES, 2 * LANES), 1)
    before = hot((source < target) | (target >= LANES))
    counts = jnp.dot(ones, before, preferred_element_type=F32)
    base = jnp.zeros((NTILE, LANES), F32)
    slot_iota = lax.broadcasted_iota(jnp.int32, (LANES, LANES), 0).astype(F32)
    for b in range(8):
        lanes = slice(b * LANES, (b + 1) * LANES)
        rank = counts[b * NTILE : (b + 1) * NTILE, :LANES] + base
        base = base + counts[b * NTILE : (b + 1) * NTILE, LANES:]
        slot = jnp.sum(jnp.where(masks[b], rank, 0.0), axis=0, keepdims=True)
        slots_ref[:, lanes] = hot(slot_iota == slot)
        for q, piece in enumerate((hi, mid, day, row, col)):
            pieces_ref[q * NTILE : (q + 1) * NTILE, lanes] = jnp.where(
                masks[b], piece[b : b + 1, :], 0.0
            ).astype(BF16)
    out = dot_nt(pieces_ref[...], slots_ref[...])
    part = [out[q * NTILE : (q + 1) * NTILE] for q in range(5)]
    send_ref[:, 0, :] = part[0] + part[1]
    send_ref[:, 1, :] = part[2] * 32768.0 + part[3] * 256.0 + part[4]


def dense(lists):
    a, b, c, d = (lists[8 * i : 8 * i + 8] for i in range(4))
    lane = lax.broadcasted_iota(jnp.int32, (8, LANES), 1)
    return jnp.concatenate(
        [
            jnp.where(lane < CAP, rows, pltpu.roll(d, shift, 1))
            for rows, shift in ((a, 96), (b, 64), (c, 32))
        ],
        axis=0,
    )


def spread_values(recv_ref, lhs_ref):
    hi, lo = split2(dense(recv_ref[:, 0, :]))
    cell = dense(recv_ref[:, 1, :]).astype(jnp.int32)
    day = jnp.right_shift(cell, 15)
    row = jnp.bitwise_and(jnp.right_shift(cell, 8), 127)
    col = jnp.bitwise_and(cell, 255)
    column = lax.broadcasted_iota(jnp.int32, (LON_DEV, LANES), 0)
    for k in range(24):
        lanes = slice(k * LANES, (k + 1) * LANES)
        here = col[k : k + 1, :] == column
        lhs_ref[:LON_DEV, lanes] = jnp.where(here, hi[k : k + 1, :], 0.0).astype(BF16)
        lhs_ref[LON_DEV:, lanes] = jnp.where(here, lo[k : k + 1, :], 0.0).astype(BF16)
    return day, row


def scatter_days(day, row, first, lhs_ref, rhs_ref):
    latitude = lax.broadcasted_iota(jnp.int32, (LAT, LANES), 0)
    for i in range(2):
        wanted = jnp.where(day == first + i, row, -1)
        for k in range(24):
            rhs_ref[i * LAT : (i + 1) * LAT, k * LANES : (k + 1) * LANES] = hot(
                wanted[k : k + 1, :] == latitude
            )
    both = dot_nt(lhs_ref[...], rhs_ref[...])
    return both[:LON_DEV] + both[LON_DEV:]


def kernel(
    tile_ref,
    cell_ref,
    value_ref,
    class_ref,
    coeff_ref,
    lag_ref,
    out_ref,
    pieces_ref,
    slots_ref,
    send_ref,
    recv_own,
    recv_prev,
    recv_next,
    class_t,
    class_halo,
    coef_ref,
    lhs_ref,
    rhs_ref,
    field,
    once,
    edge_own,
    edge_halo,
    got_own,
    got_halo,
    mix_ref,
    smooth_hi,
    smooth_lo,
    list_send,
    list_recv,
    year_send,
    year_recv,
    class_send,
    class_recv,
    edge_send,
    edge_recv,
):
    segment = lax.axis_index("year")
    me = lax.axis_index("tile")
    after = lax.rem(segment + 1, NYEAR)
    ahead = lax.rem(segment + NYEAR - 1, NYEAR)
    east = lax.rem(me + 1, NTILE)
    west = lax.rem(me + NTILE - 1, NTILE)

    barrier = pltpu.get_barrier_semaphore()

    @pl.loop(1, NTILE)
    def _(i):
        pl.semaphore_signal(barrier, inc=1, device_id={"tile": lax.rem(me + i, NTILE)})

    pl.semaphore_signal(barrier, inc=1, device_id={"year": after})
    pl.semaphore_signal(barrier, inc=1, device_id={"year": ahead})

    bucket(tile_ref, cell_ref, value_ref, pieces_ref, slots_ref, send_ref)
    class_t[...] = jnp.transpose(class_ref[...])

    pl.semaphore_wait(barrier, NTILE + 1)

    @pl.loop(1, NTILE)
    def _(i):
        tgt = lax.rem(me + i, NTILE)
        pltpu.make_async_remote_copy(
            send_ref.at[tgt], recv_own.at[i], list_send, list_recv, device_id={"tile": tgt}
        ).start()

    recv_own[0] = send_ref[me]
    class_copies = [
        pltpu.make_async_remote_copy(
            class_t.at[pl.ds(start, PAD)],
            class_halo.at[1 - side],
            class_send.at[side],
            class_recv.at[1 - side],
            device_id={"tile": tgt},
        )
        for side, start, tgt in ((0, 0, west), (1, LON_DEV - PAD, east))
    ]
    for copy in class_copies:
        copy.start()

    mix_ref[...] = jnp.zeros_like(mix_ref)
    for k in range(LAGS):
        hi, lo = split2(lag_ref[k])
        for i in range(2):
            lanes = slice((k + i) * LAT, (k + i + 1) * LAT)
            mix_ref[i * LAT : (i + 1) * LAT, lanes] = hi.astype(BF16)
            mix_ref[(2 + i) * LAT : (3 + i) * LAT, lanes] = lo.astype(BF16)

    def coefficients(ids, rows):
        kappa = hzon = hmer = jnp.zeros(ids.shape, F32)
        for c in range(NCLASS):
            here = ids == c
            kappa = jnp.where(here, coeff_ref[0, c], kappa)
            hzon = jnp.where(here, coeff_ref[1, c], hzon)
            hmer = jnp.where(here, coeff_ref[2, c], hmer)
        lane = lax.broadcasted_iota(jnp.int32, ids.shape, 1)
        coef_ref[0, rows] = kappa + 2.0 * hzon + 2.0 * hmer
        coef_ref[1, rows] = hzon
        coef_ref[2, rows] = jnp.where(lane < LAT - 1, hmer, 0.0)
        coef_ref[3, rows] = jnp.where(lane > 0, hmer, 0.0)

    coefficients(class_t[...], slice(PAD, PAD + LON_DEV))
    for copy in class_copies:
        copy.wait()
    coefficients(class_halo[0], slice(0, PAD))
    coefficients(class_halo[1], slice(PAD + LON_DEV, 2 * PAD + LON_DEV))

    everything = pltpu.make_async_remote_copy(
        send_ref.at[pl.ds(1, NTILE - 1)],
        recv_own.at[pl.ds(1, NTILE - 1)],
        list_send,
        list_recv,
        device_id={"tile": east},
    )
    everything.wait_recv()
    year_copies = [
        pltpu.make_async_remote_copy(
            recv_own, target, year_send.at[i], year_recv.at[i], device_id={"year": tgt}
        )
        for i, (target, tgt) in enumerate(((recv_prev, after), (recv_next, ahead)))
    ]
    for copy in year_copies:
        copy.start()

    def place(both, first, edges, at):
        for i in range(2):
            plane = both[:, i * LAT : (i + 1) * LAT]
            field[first + i, PAD : PAD + LON_DEV] = plane
            edges[0, at + 2 * i : at + 2 * i + 2] = plane[:2]
            edges[1, at + 2 * i : at + 2 * i + 2] = plane[LON_DEV - 2 :]

    def exchange(edges, got, which):
        copies = [
            pltpu.make_async_remote_copy(
                edges.at[side],
                got.at[1 - side],
                edge_send.at[which, side],
                edge_recv.at[which, 1 - side],
                device_id={"tile": tgt},
            )
            for side, tgt in ((0, west), (1, east))
        ]
        for copy in copies:
            copy.start()
        return copies

    day, row = spread_values(recv_own, lhs_ref)
    for pair in range(DAY_DEV // 2):
        both = scatter_days(day, row, 2 * pair, lhs_ref, rhs_ref)
        place(both, HALO + 2 * pair, edge_own, 4 * pair)
    own_copies = exchange(edge_own, got_own, 0)
    for i, (source, days, first) in enumerate(
        ((recv_prev, DAY_DEV - HALO, 0), (recv_next, 0, HALO + DAY_DEV))
    ):
        year_copies[i].wait_recv()
        day, row = spread_values(source, lhs_ref)
        place(scatter_days(day, row, days, lhs_ref, rhs_ref), first, edge_halo, 4 * i)
    halo_copies = exchange(edge_halo, got_halo, 1)

    def stencil(src, at, rows):
        length = rows.stop - rows.start
        v = src[at + (rows,)]
        e = src[at + (slice(rows.start + 1, rows.stop + 1),)]
        w = src[at + (slice(rows.start - 1, rows.stop - 1),)]
        north = pltpu.roll(v, LAT - 1, 1)
        south = pltpu.roll(v, 1, 1)
        return (
            coef_ref[0, rows] * v
            - coef_ref[1, rows] * (e + w)
            - coef_ref[2, rows] * north
            - coef_ref[3, rows] * south
        )

    def smooth(e, got, at):
        field[e, PAD - 2 : PAD] = got[0, at : at + 2]
        field[e, PAD + LON_DEV : PAD + LON_DEV + 2] = got[1, at : at + 2]
        for rows in (
            slice(PAD, PAD + LON_DEV),
            slice(PAD - 1, PAD),
            slice(PAD + LON_DEV, PAD + LON_DEV + 1),
        ):
            once[rows] = stencil(field, (e,), rows)
        twice = stencil(once, (), slice(PAD, PAD + LON_DEV))
        hi, lo = split2(twice)
        smooth_hi[:, e * LAT : (e + 1) * LAT] = hi.astype(BF16)
        smooth_lo[:, e * LAT : (e + 1) * LAT] = lo.astype(BF16)

    for copy in own_copies:
        copy.wait()
    for d in range(DAY_DEV):
        smooth(HALO + d, got_own, 2 * d)
    for copy in halo_copies:
        copy.wait()
    for i, e in enumerate((0, 1, HALO + DAY_DEV, HALO + DAY_DEV + 1)):
        smooth(e, got_halo, 2 * i)

    for pair in range(DAY_DEV // 2):
        window = slice(2 * pair * LAT, (2 * pair + LAGS + 1) * LAT)
        first = dot_nt(mix_ref[...], smooth_hi[:, window])
        second = dot_nt(mix_ref[: 2 * LAT], smooth_lo[:, window])
        mixed = first[: 2 * LAT] + (first[2 * LAT :] + second)
        out_ref[2 * pair] = mixed[:LAT]
        out_ref[2 * pair + 1] = mixed[LAT:]

    everything.wait_send()
    for copy in year_copies:
        copy.wait_send()


def body(station_tile, station_cell, station_value, class_ids, coeff_table, lag_blocks):
    vmem = pl.BlockSpec(memory_space=pltpu.VMEM)
    smem = pl.BlockSpec(memory_space=pltpu.SMEM)
    dma = pltpu.SemaphoreType.DMA
    slots = NTILE * CAP
    return pl.pallas_call(
        kernel,
        out_shape=jax.ShapeDtypeStruct((DAY_DEV, LAT, LON_DEV), F32),
        in_specs=[vmem, vmem, vmem, vmem, smem, vmem],
        out_specs=vmem,
        scratch_shapes=[
            pltpu.VMEM((5 * NTILE, 8 * LANES), BF16),
            pltpu.VMEM((LANES, 8 * LANES), BF16),
            pltpu.VMEM((NTILE, 2, LANES), F32),
            pltpu.VMEM((NTILE, 2, LANES), F32),
            pltpu.VMEM((NTILE, 2, LANES), F32),
            pltpu.VMEM((NTILE, 2, LANES), F32),
            pltpu.VMEM((LON_DEV, LAT), jnp.int32),
            pltpu.VMEM((2, PAD, LAT), jnp.int32),
            pltpu.VMEM((4, LON_DEV + 2 * PAD, LAT), F32),
            pltpu.VMEM((2 * LON_DEV, slots), BF16),
            pltpu.VMEM((2 * LAT, slots), BF16),
            pltpu.VMEM((DAYS_EXT, LON_DEV + 2 * PAD, LAT), F32),
            pltpu.VMEM((LON_DEV + 2 * PAD, LAT), F32),
            pltpu.VMEM((2, 2 * DAY_DEV, LAT), F32),
            pltpu.VMEM((2, 4 * HALO, LAT), F32),
            pltpu.VMEM((2, 2 * DAY_DEV, LAT), F32),
            pltpu.VMEM((2, 4 * HALO, LAT), F32),
            pltpu.VMEM((4 * LAT, (LAGS + 1) * LAT), BF16),
            pltpu.VMEM((LON_DEV, DAYS_EXT * LAT), BF16),
            pltpu.VMEM((LON_DEV, DAYS_EXT * LAT), BF16),
            dma,
            dma,
            dma((2,)),
            dma((2,)),
            dma((2,)),
            dma((2,)),
            dma((2, 2)),
            dma((2, 2)),
        ],
        compiler_params=pltpu.CompilerParams(
            collective_id=0, has_side_effects=True, vmem_limit_bytes=40 * 2**20
        ),
    )(
        station_tile.reshape(8, LANES),
        station_cell.reshape(8, LANES),
        station_value.reshape(8, LANES),
        class_ids,
        coeff_table,
        lag_blocks,
    )


def solution(mesh):
    in_specs = (
        P(("year", "tile"), None),
        P(("year", "tile")),
        P(("year", "tile")),
        P(None, "tile"),
        P(),
        P(),
    )
    out_specs = P("year", None, "tile")
    return jax.shard_map(body, mesh=mesh, in_specs=in_specs, out_specs=out_specs, check_vma=False)
```

```python
import jax
import jax.numpy as jnp
from jax import lax
from jax.experimental import pallas as pl
from jax.experimental.pallas import tpu as pltpu
from jax.sharding import PartitionSpec as P

DAY_DEV = 8
LAT = 128
LON_DEV = 256
CAP = 96
LANES = 128
NTILE = 32
NYEAR = 4
NCLASS = 16
GROUPS = ((0, 8), (8, 8), (16, 8), (24, 8))
FAR_PARTS = ((0, 16), (16, 16))
MOST = 16
LAGS = 5
HALO = 2
DAYS_EXT = DAY_DEV + 2 * HALO
PAD = 8
F32 = jnp.float32
BF16 = jnp.bfloat16


def dot_nt(a, b):
    return lax.dot_general(a, b, (((1,), (1,)), ((), ())), preferred_element_type=F32)


def split2(x):
    hi = x.astype(BF16).astype(F32)
    return hi, x - hi


def hot(mask):
    return jnp.where(mask, 1.0, 0.0).astype(BF16)


def hops(offset):
    return sum(min(o, n - o) * step for o, n, step in zip(offset, (4, 2, 4), (1, 2, 1)))


OFFSETS = sorted(((x, z, y) for x in range(4) for z in range(2) for y in range(4)), key=hops)


def bucket(tile, cell, value, pieces_ref, slots_ref, send_ref):
    hi, mid = split2(value)
    day = jnp.right_shift(cell, 15).astype(F32)
    row = jnp.bitwise_and(jnp.right_shift(cell, 8), 127).astype(F32)
    col = jnp.bitwise_and(cell, 255).astype(F32)
    of_tile = lax.broadcasted_iota(jnp.int32, (NTILE, LANES), 0)
    masks = [tile[b : b + 1, :] == of_tile for b in range(8)]
    ones = jnp.concatenate([hot(m) for m in masks], axis=0)
    source = lax.broadcasted_iota(jnp.int32, (LANES, 2 * LANES), 0)
    target = lax.broadcasted_iota(jnp.int32, (LANES, 2 * LANES), 1)
    before = hot((source < target) | (target >= LANES))
    counts = jnp.dot(ones, before, preferred_element_type=F32)
    base = jnp.zeros((NTILE, LANES), F32)
    slot_iota = lax.broadcasted_iota(jnp.int32, (LANES, LANES), 0).astype(F32)
    for b in range(8):
        lanes = slice(b * LANES, (b + 1) * LANES)
        rank = counts[b * NTILE : (b + 1) * NTILE, :LANES] + base
        base = base + counts[b * NTILE : (b + 1) * NTILE, LANES:]
        slot = jnp.sum(jnp.where(masks[b], rank, 0.0), axis=0, keepdims=True)
        slots_ref[:, lanes] = hot(slot_iota == slot)
        for q, piece in enumerate((hi, mid, day, row, col)):
            pieces_ref[q * NTILE : (q + 1) * NTILE, lanes] = jnp.where(
                masks[b], piece[b : b + 1, :], 0.0
            ).astype(BF16)
    out = dot_nt(pieces_ref[...], slots_ref[...])
    part = [out[q * NTILE : (q + 1) * NTILE] for q in range(5)]
    values = part[0] + part[1]
    cells = part[2] * 32768.0 + part[3] * 256.0 + part[4]
    for q, x in enumerate((values, cells)):
        send_ref[1 : NTILE + 1, q, :] = x
        send_ref[0:1, q, :] = x[NTILE - 1 :]
        send_ref[NTILE + 1 : NTILE + 2, q, :] = x[:1]


def dense(lists):
    lane = lax.broadcasted_iota(jnp.int32, (1, LANES), 1)
    turned = [pltpu.roll(lists, shift, 1) for shift in (96, 64, 32)]
    return [
        jnp.where(lane < CAP, lists[i + j : i + j + 1], turned[j][i + 3 : i + 4])
        for i in range(0, lists.shape[0], 4)
        for j in range(3)
    ]


def entries(recv_ref, senders, which):
    at = slice(senders[0], sum(senders))
    hi, lo = split2(recv_ref[at, which, 0, :])
    return hi, lo, recv_ref[at, which, 1, :].astype(jnp.int32)


def scatter(recv_ref, senders, days, lhs_ref, rhs_ref, field, first):
    hi, lo, cell = entries(recv_ref, senders, 1)
    hi, lo = dense(hi), dense(lo)
    col = dense(jnp.bitwise_and(cell, 255))
    plane = dense(jnp.right_shift(cell, 8))
    depth = len(col) * LANES
    column = lax.broadcasted_iota(jnp.int32, (LON_DEV, LANES), 0)
    latitude = lax.broadcasted_iota(jnp.int32, (LAT, LANES), 0)
    for k in range(len(col)):
        lanes = slice(k * LANES, (k + 1) * LANES)
        here = col[k] == column
        lhs_ref[:LON_DEV, lanes] = jnp.where(here, hi[k], 0.0).astype(BF16)
        lhs_ref[LON_DEV:, lanes] = jnp.where(here, lo[k], 0.0).astype(BF16)
    for i, d in enumerate(days):
        for k in range(len(col)):
            rhs_ref[i * LAT : (i + 1) * LAT, k * LANES : (k + 1) * LANES] = hot(
                plane[k] - d * LAT == latitude
            )
    for pair in range(len(days) // 2):
        both = dot_nt(
            lhs_ref[:, :depth], rhs_ref[2 * LAT * pair : 2 * LAT * (pair + 1), :depth]
        )
        both = both[:LON_DEV] + both[LON_DEV:]
        for i in range(2):
            part = both[:, i * LAT : (i + 1) * LAT]
            e = first + 2 * pair + i
            if senders[0] == 0:
                field[e, PAD : PAD + LON_DEV] = part
            else:
                field[e, PAD : PAD + LON_DEV] += part


def scatter_edges(recv_ref, senders, count, number_of, lhs_ref, rhs_ref, edges, first):
    rows = 4 * count
    latitude = lax.broadcasted_iota(jnp.int32, (LAT, LANES), 0)
    number = lax.broadcasted_iota(jnp.int32, (rows, LANES), 0)
    blocks = 3 * senders[1] // 4
    for j, which in enumerate((0, 2)):
        hi, lo, cell = entries(recv_ref, senders, which)
        col = jnp.bitwise_and(cell, 255)
        near = col >= LON_DEV - 2 if which == 0 else col < 2
        place = 4 * number_of(jnp.right_shift(cell, 15)) + (
            col - (LON_DEV - 2) if which == 0 else col + 2
        )
        place = dense(jnp.where(near, place, -1))
        lat = dense(jnp.bitwise_and(jnp.right_shift(cell, 8), LAT - 1))
        hi, lo = dense(hi), dense(lo)
        for k in range(blocks):
            lanes = slice((blocks * j + k) * LANES, (blocks * j + k + 1) * LANES)
            here = place[k] == number
            lhs_ref[:rows, lanes] = jnp.where(here, hi[k], 0.0).astype(BF16)
            lhs_ref[rows : 2 * rows, lanes] = jnp.where(here, lo[k], 0.0).astype(BF16)
            rhs_ref[:, lanes] = hot(lat[k] == latitude)
    depth = 2 * blocks * LANES
    both = dot_nt(lhs_ref[: 2 * rows, :depth], rhs_ref[:, :depth])
    both = both[:rows] + both[rows:]
    for i in range(count):
        if senders[0] == 0:
            edges[first + i] = both[4 * i : 4 * i + 4]
        else:
            edges[first + i] += both[4 * i : 4 * i + 4]


def kernel(
    tile_hbm,
    cell_hbm,
    value_hbm,
    class_hbm,
    coeff_hbm,
    lag_hbm,
    out_ref,
    tile_ref,
    cell_ref,
    value_ref,
    class_ref,
    coeff_ref,
    lag_ref,
    pieces_ref,
    slots_ref,
    send_ref,
    recv_own,
    recv_far,
    class_t,
    class_halo,
    coef_ref,
    lhs_ref,
    rhs_ref,
    edge_lhs,
    edge_rhs,
    field,
    edges,
    once,
    mix_ref,
    smooth_hi,
    smooth_lo,
    near_out,
    near_in,
    load_sem,
    list_send,
    list_recv,
    far_send,
    far_recv,
    near_send,
    near_recv,
    class_send,
    class_recv,
):
    loads = [
        pltpu.make_async_copy(source, target, load_sem.at[i])
        for i, (source, target) in enumerate(
            (
                (tile_hbm, tile_ref),
                (cell_hbm, cell_ref),
                (value_hbm, value_ref),
                (class_hbm, class_ref),
                (coeff_hbm, coeff_ref),
                (lag_hbm, lag_ref),
            )
        )
    ]
    for load in loads[:3]:
        load.start()

    segment = lax.axis_index("year")
    me = lax.axis_index("tile")
    odd = lax.rem(segment, 2)
    near = segment + 1 - 2 * odd
    far = lax.rem(segment + NYEAR - 1 + 2 * odd, NYEAR)

    def day_of(d):
        return d + odd * (DAY_DEV - 1 - 2 * d)

    east = lax.rem(me + 1, NTILE)
    west = lax.rem(me + NTILE - 1, NTILE)
    x, z, y = me // 8, lax.rem(me // 4, 2), lax.rem(me, 4)
    peers = [
        lax.rem(x + dx, 4) * 8 + lax.rem(z + dz, 2) * 4 + lax.rem(y + dy, 4)
        for dx, dz, dy in OFFSETS
    ]

    barrier = pltpu.get_barrier_semaphore()
    for i in reversed(range(1, NTILE)):
        pl.semaphore_signal(barrier, inc=1, device_id={"tile": peers[i]})
    pl.semaphore_signal(barrier, inc=1, device_id={"year": near})
    pl.semaphore_signal(barrier, inc=1, device_id={"year": far})
    for load in loads[3:]:
        load.start()

    for load in loads[:3]:
        load.wait()
    bucket(tile_ref[...], cell_ref[...], value_ref[...], pieces_ref, slots_ref, send_ref)

    pl.semaphore_wait(barrier, NTILE + 1)

    for g, (low, count) in reversed(list(enumerate(GROUPS))):
        for i in reversed(range(max(low, 1), low + count)):
            pltpu.make_async_remote_copy(
                send_ref.at[pl.ds(peers[i], 3)],
                recv_own.at[i],
                list_send,
                list_recv.at[g],
                device_id={"tile": peers[i]},
            ).start()
    recv_own[0] = send_ref[pl.ds(me, 3)]
    loads[3].wait()
    class_t[...] = jnp.transpose(class_ref[...])
    class_copies = [
        pltpu.make_async_remote_copy(
            class_t.at[pl.ds(start, PAD)],
            class_halo.at[1 - side],
            class_send.at[side],
            class_recv.at[1 - side],
            device_id={"tile": tgt},
        )
        for side, start, tgt in ((0, 0, west), (1, LON_DEV - PAD, east))
    ]
    for copy in class_copies:
        copy.start()

    loads[4].wait()
    loads[5].wait()
    mix_ref[...] = jnp.zeros_like(mix_ref)
    for k in range(LAGS):
        hi, lo = split2(lag_ref[k + odd * (LAGS - 1 - 2 * k)])
        for i in range(2):
            lanes = slice((k + i) * LAT, (k + i + 1) * LAT)
            mix_ref[i * LAT : (i + 1) * LAT, lanes] = hi.astype(BF16)
            mix_ref[(2 + i) * LAT : (3 + i) * LAT, lanes] = lo.astype(BF16)

    def coefficients(ids, rows):
        kappa = hzon = hmer = jnp.zeros(ids.shape, F32)
        for c in range(NCLASS):
            here = ids == c
            kappa = jnp.where(here, coeff_ref[0, c], kappa)
            hzon = jnp.where(here, coeff_ref[1, c], hzon)
            hmer = jnp.where(here, coeff_ref[2, c], hmer)
        lane = lax.broadcasted_iota(jnp.int32, ids.shape, 1)
        coef_ref[0, rows] = kappa + 2.0 * hzon + 2.0 * hmer
        coef_ref[1, rows] = hzon
        coef_ref[2, rows] = jnp.where(lane < LAT - 1, hmer, 0.0)
        coef_ref[3, rows] = jnp.where(lane > 0, hmer, 0.0)

    coefficients(class_t[...], slice(PAD, PAD + LON_DEV))

    forwarded = []

    def own(group):
        start, count = GROUPS[group]
        low = max(1, start)
        pltpu.make_async_remote_copy(
            recv_own.at[pl.ds(low, start + count - low)],
            recv_own.at[pl.ds(low, start + count - low)],
            list_send,
            list_recv.at[group],
            device_id={"tile": east},
        ).wait_recv()
        copy = pltpu.make_async_remote_copy(
            recv_own.at[pl.ds(start, count)],
            recv_far.at[pl.ds(start, count)],
            far_send.at[group],
            far_recv.at[group],
            device_id={"year": far},
        )
        copy.start()
        forwarded.append(copy)
        days = [day_of(d) for d in range(DAY_DEV)]
        scatter(recv_own, GROUPS[group], days, lhs_ref, rhs_ref, field, HALO)
        scatter_edges(
            recv_own, GROUPS[group], DAY_DEV, day_of, edge_lhs, edge_rhs, edges, HALO
        )

    def halo(part):
        senders = FAR_PARTS[part]
        for group, (start, _) in enumerate(GROUPS):
            if senders[0] <= start < sum(senders):
                forwarded[group].wait_recv()
        days = [day_of(d + DAY_DEV - HALO) for d in range(HALO)]
        scatter(recv_far, senders, days, lhs_ref, rhs_ref, field, 0)
        scatter_edges(
            recv_far,
            senders,
            HALO,
            lambda day: day_of(day) - (DAY_DEV - HALO),
            edge_lhs,
            edge_rhs,
            edges,
            0,
        )

    def stencil(src, at, rows):
        v = src[at + (rows,)]
        e = src[at + (slice(rows.start + 1, rows.stop + 1),)]
        w = src[at + (slice(rows.start - 1, rows.stop - 1),)]
        north = pltpu.roll(v, LAT - 1, 1)
        south = pltpu.roll(v, 1, 1)
        return (
            coef_ref[0, rows] * v
            - coef_ref[1, rows] * (e + w)
            - coef_ref[2, rows] * north
            - coef_ref[3, rows] * south
        )

    def keep(e, plane):
        hi, lo = split2(plane)
        smooth_hi[e] = hi.astype(BF16)
        smooth_lo[e] = lo.astype(BF16)

    def smooth(e):
        field[e, PAD - 2 : PAD] = edges[e, :2]
        field[e, PAD + LON_DEV : PAD + LON_DEV + 2] = edges[e, 2:]
        for rows in (
            slice(PAD, PAD + LON_DEV),
            slice(PAD - 1, PAD),
            slice(PAD + LON_DEV, PAD + LON_DEV + 1),
        ):
            once[rows] = stencil(field, (e,), rows)
        twice = stencil(once, (), slice(PAD, PAD + LON_DEV))
        keep(e, twice)
        return twice

    def mix(pair):
        window = range(2 * pair, 2 * pair + LAGS + 1)
        hi = jnp.concatenate([smooth_hi[e] for e in window], axis=1)
        lo = jnp.concatenate([smooth_lo[e] for e in window], axis=1)
        first = dot_nt(mix_ref[...], hi)
        second = dot_nt(mix_ref[: 2 * LAT], lo)
        mixed = first[: 2 * LAT] + (first[2 * LAT :] + second)
        out_ref[day_of(2 * pair)] = mixed[:LAT]
        out_ref[day_of(2 * pair + 1)] = mixed[LAT:]

    own(0)
    own(1)
    for copy in class_copies:
        copy.wait()
    coefficients(class_halo[0], slice(0, PAD))
    coefficients(class_halo[1], slice(PAD + LON_DEV, 2 * PAD + LON_DEV))
    own(2)
    halo(0)
    own(3)
    near_copies = []
    for i, e in enumerate((HALO + DAY_DEV - 1, HALO + DAY_DEV - 2)):
        near_out[i] = smooth(e)
        copy = pltpu.make_async_remote_copy(
            near_out.at[i], near_in.at[i], near_send.at[i], near_recv.at[i], device_id={"year": near}
        )
        copy.start()
        near_copies.append(copy)
    for d in range(DAY_DEV - 2):
        smooth(HALO + d)
    mix(1)
    mix(2)
    for i, copy in enumerate(near_copies):
        copy.wait()
        keep(HALO + DAY_DEV + i, near_in[i])
    mix(3)
    halo(1)
    smooth(1)
    smooth(0)
    mix(0)

    pltpu.make_async_remote_copy(
        recv_own.at[pl.ds(1, NTILE - 1)],
        recv_own.at[pl.ds(1, NTILE - 1)],
        list_send,
        list_recv.at[0],
        device_id={"tile": east},
    ).wait_send()
    for copy in forwarded:
        copy.wait_send()


def body(station_tile, station_cell, station_value, class_ids, coeff_table, lag_blocks):
    hbm = pl.BlockSpec(memory_space=pltpu.HBM)
    dma = pltpu.SemaphoreType.DMA
    groups = len(GROUPS)
    return pl.pallas_call(
        kernel,
        out_shape=pltpu.VMEM((DAY_DEV, LAT, LON_DEV), F32),
        in_specs=[hbm] * 6,
        out_specs=pl.BlockSpec(memory_space=pltpu.VMEM),
        scratch_shapes=[
            pltpu.VMEM((8, LANES), jnp.int32),
            pltpu.VMEM((8, LANES), jnp.int32),
            pltpu.VMEM((8, LANES), F32),
            pltpu.VMEM((LAT, LON_DEV), jnp.int32),
            pltpu.SMEM((3, NCLASS), F32),
            pltpu.VMEM((LAGS, LAT, LAT), F32),
            pltpu.VMEM((5 * NTILE, 8 * LANES), BF16),
            pltpu.VMEM((LANES, 8 * LANES), BF16),
            pltpu.VMEM((NTILE + 2, 2, LANES), F32),
            pltpu.VMEM((NTILE, 3, 2, LANES), F32),
            pltpu.VMEM((NTILE, 3, 2, LANES), F32),
            pltpu.VMEM((LON_DEV, LAT), jnp.int32),
            pltpu.VMEM((2, PAD, LAT), jnp.int32),
            pltpu.VMEM((4, LON_DEV + 2 * PAD, LAT), F32),
            pltpu.VMEM((2 * LON_DEV, MOST * CAP), BF16),
            pltpu.VMEM((DAY_DEV * LAT, MOST * CAP), BF16),
            pltpu.VMEM((8 * DAY_DEV, 2 * MOST * CAP), BF16),
            pltpu.VMEM((LAT, 2 * MOST * CAP), BF16),
            pltpu.VMEM((DAYS_EXT, LON_DEV + 2 * PAD, LAT), F32),
            pltpu.VMEM((DAYS_EXT, 4, LAT), F32),
            pltpu.VMEM((LON_DEV + 2 * PAD, LAT), F32),
            pltpu.VMEM((4 * LAT, (LAGS + 1) * LAT), BF16),
            pltpu.VMEM((DAYS_EXT, LON_DEV, LAT), BF16),
            pltpu.VMEM((DAYS_EXT, LON_DEV, LAT), BF16),
            pltpu.VMEM((HALO, LON_DEV, LAT), F32),
            pltpu.VMEM((HALO, LON_DEV, LAT), F32),
            dma((6,)),
            dma,
            dma((groups,)),
            dma((groups,)),
            dma((groups,)),
            dma((HALO,)),
            dma((HALO,)),
            dma((2,)),
            dma((2,)),
        ],
        compiler_params=pltpu.CompilerParams(
            collective_id=0, has_side_effects=True, vmem_limit_bytes=40 * 2**20
        ),
    )(
        *(
            pltpu.with_memory_space_constraint(x, pltpu.HBM)
            for x in (
                station_tile.reshape(8, LANES),
                station_cell.reshape(8, LANES),
                station_value.reshape(8, LANES),
                class_ids,
                coeff_table,
                lag_blocks,
            )
        )
    )


def solution(mesh):
    in_specs = (
        P(("year", "tile"), None),
        P(("year", "tile")),
        P(("year", "tile")),
        P(None, "tile"),
        P(),
        P(),
    )
    out_specs = P("year", None, "tile")
    return jax.shard_map(body, mesh=mesh, in_specs=in_specs, out_specs=out_specs, check_vma=False)
```

```python
import jax
import jax.numpy as jnp
from jax import lax
from jax.experimental import pallas as pl
from jax.experimental.pallas import tpu as pltpu
from jax.sharding import PartitionSpec as P

DAY_DEV = 8
LAT = 128
LON_DEV = 256
CAP = 96
LANES = 128
NTILE = 32
NYEAR = 4
NCLASS = 16
GROUPS = ((0, 16), (16, 16))
FAR_PARTS = ((0, 32),)
MOST = 32
LAGS = 5
HALO = 2
DAYS_EXT = DAY_DEV + 2 * HALO
PAD = 8
F32 = jnp.float32
BF16 = jnp.bfloat16


def dot_nt(a, b):
    return lax.dot_general(a, b, (((1,), (1,)), ((), ())), preferred_element_type=F32)


def split2(x):
    hi = x.astype(BF16).astype(F32)
    return hi, x - hi


def hot(mask):
    return jnp.where(mask, 1.0, 0.0).astype(BF16)


def hops(offset):
    return sum(min(o, n - o) * step for o, n, step in zip(offset, (4, 2, 4), (1, 2, 1)))


OFFSETS = sorted(((x, z, y) for x in range(4) for z in range(2) for y in range(4)), key=hops)


def spread(row, count):
    few = jnp.broadcast_to(row.astype(F32), (16, LANES)).astype(BF16)
    return jnp.concatenate([few] * (count // 16), axis=0)


def numbers(count):
    return lax.broadcasted_iota(jnp.int32, (count, LANES), 0).astype(F32).astype(BF16)


def pick(row, iota, piece=None):
    count = iota.shape[0]
    value = jnp.ones((), BF16) if piece is None else spread(piece, count)
    return jnp.where(spread(row, count) == iota, value, jnp.zeros((), BF16))


def bucket(tile, cell, value, pieces_ref, slots_ref, send_ref):
    hi, mid = split2(value)
    day = jnp.right_shift(cell, 15).astype(F32)
    row = jnp.bitwise_and(jnp.right_shift(cell, 8), 127).astype(F32)
    col = jnp.bitwise_and(cell, 255).astype(F32)
    of_tile = lax.broadcasted_iota(jnp.int32, (NTILE, LANES), 0)
    masks = [tile[b : b + 1, :] == of_tile for b in range(8)]
    ones = jnp.concatenate([hot(m) for m in masks], axis=0)
    source = lax.broadcasted_iota(jnp.int32, (LANES, 2 * LANES), 0)
    target = lax.broadcasted_iota(jnp.int32, (LANES, 2 * LANES), 1)
    before = hot((source < target) | (target >= LANES))
    counts = jnp.dot(ones, before, preferred_element_type=F32)
    base = jnp.zeros((NTILE, LANES), F32)
    slot_iota = lax.broadcasted_iota(jnp.int32, (LANES, LANES), 0).astype(F32)
    for b in range(8):
        lanes = slice(b * LANES, (b + 1) * LANES)
        rank = counts[b * NTILE : (b + 1) * NTILE, :LANES] + base
        base = base + counts[b * NTILE : (b + 1) * NTILE, LANES:]
        slot = jnp.sum(jnp.where(masks[b], rank, 0.0), axis=0, keepdims=True)
        slots_ref[:, lanes] = hot(slot_iota == slot)
        for q, piece in enumerate((hi, mid, day, row, col)):
            pieces_ref[q * NTILE : (q + 1) * NTILE, lanes] = jnp.where(
                masks[b], piece[b : b + 1, :], 0.0
            ).astype(BF16)
    out = dot_nt(pieces_ref[...], slots_ref[...])
    part = [out[q * NTILE : (q + 1) * NTILE] for q in range(5)]
    values = part[0] + part[1]
    cells = part[2] * 32768.0 + part[3] * 256.0 + part[4]
    for q, x in enumerate((values, cells)):
        send_ref[1 : NTILE + 1, q, :] = x
        send_ref[0:1, q, :] = x[NTILE - 1 :]
        send_ref[NTILE + 1 : NTILE + 2, q, :] = x[:1]


def dense(lists):
    lane = lax.broadcasted_iota(jnp.int32, (1, LANES), 1)
    turned = [pltpu.roll(lists, shift, 1) for shift in (96, 64, 32)]
    return [
        jnp.where(lane < CAP, lists[i + j : i + j + 1], turned[j][i + 3 : i + 4])
        for i in range(0, lists.shape[0], 4)
        for j in range(3)
    ]


def entries(recv_ref, senders, which):
    at = slice(senders[0], sum(senders))
    if len(recv_ref.shape) == 3:
        value, cell = recv_ref[at, 0, :], recv_ref[at, 1, :]
    else:
        value, cell = recv_ref[at, which, 0, :], recv_ref[at, which, 1, :]
    hi, lo = split2(value)
    return hi, lo, cell.astype(jnp.int32)


def scatter(recv_ref, senders, days, lhs_ref, rhs_ref, field, first):
    hi, lo, cell = entries(recv_ref, senders, 1)
    hi, lo = dense(hi), dense(lo)
    col = dense(jnp.bitwise_and(cell, 255))
    plane = dense(jnp.right_shift(cell, 8))
    depth = len(col) * LANES
    column, latitude = numbers(LON_DEV), numbers(LAT)
    for k in range(len(col)):
        lanes = slice(k * LANES, (k + 1) * LANES)
        lhs_ref[:LON_DEV, lanes] = pick(col[k], column, hi[k])
        lhs_ref[LON_DEV:, lanes] = pick(col[k], column, lo[k])
    for i, d in enumerate(days):
        for k in range(len(col)):
            rhs_ref[i * LAT : (i + 1) * LAT, k * LANES : (k + 1) * LANES] = pick(
                plane[k] - d * LAT, latitude
            )
    for pair in range(len(days) // 2):
        both = dot_nt(
            lhs_ref[:, :depth], rhs_ref[2 * LAT * pair : 2 * LAT * (pair + 1), :depth]
        )
        both = both[:LON_DEV] + both[LON_DEV:]
        for i in range(2):
            part = both[:, i * LAT : (i + 1) * LAT]
            e = first + 2 * pair + i
            if senders[0] == 0:
                field[e, PAD : PAD + LON_DEV] = part
            else:
                field[e, PAD : PAD + LON_DEV] += part


def scatter_edges(recv_ref, senders, count, number_of, lhs_ref, rhs_ref, edges, first):
    rows = 4 * count
    padded = max(rows, 16)
    latitude, number = numbers(LAT), numbers(padded)
    blocks = 3 * senders[1] // 4
    for j, which in enumerate((0, 2)):
        hi, lo, cell = entries(recv_ref, senders, which)
        col = jnp.bitwise_and(cell, 255)
        near = col >= LON_DEV - 2 if which == 0 else col < 2
        place = 4 * number_of(jnp.right_shift(cell, 15)) + (
            col - (LON_DEV - 2) if which == 0 else col + 2
        )
        place = dense(jnp.where(near, place, -1))
        lat = dense(jnp.bitwise_and(jnp.right_shift(cell, 8), LAT - 1))
        hi, lo = dense(hi), dense(lo)
        for k in range(blocks):
            lanes = slice((blocks * j + k) * LANES, (blocks * j + k + 1) * LANES)
            lhs_ref[:padded, lanes] = pick(place[k], number, hi[k])
            lhs_ref[padded : 2 * padded, lanes] = pick(place[k], number, lo[k])
            rhs_ref[:, lanes] = pick(lat[k], latitude)
    depth = 2 * blocks * LANES
    both = dot_nt(lhs_ref[: 2 * padded, :depth], rhs_ref[:, :depth])
    both = both[:padded] + both[padded:]
    for i in range(count):
        if senders[0] == 0:
            edges[first + i] = both[4 * i : 4 * i + 4]
        else:
            edges[first + i] += both[4 * i : 4 * i + 4]


def kernel(
    tile_hbm,
    cell_hbm,
    value_hbm,
    class_hbm,
    coeff_hbm,
    lag_hbm,
    out_ref,
    tile_ref,
    cell_ref,
    value_ref,
    class_ref,
    coeff_ref,
    lag_ref,
    pieces_ref,
    slots_ref,
    send_ref,
    recv_own,
    recv_far,
    class_t,
    class_halo,
    coef_ref,
    lhs_ref,
    rhs_ref,
    edge_lhs,
    edge_rhs,
    field,
    edges,
    once,
    mix_ref,
    smooth_hi,
    smooth_lo,
    near_out,
    near_in,
    load_sem,
    list_send,
    list_recv,
    far_send,
    far_recv,
    near_send,
    near_recv,
    edge_send,
    edge_recv,
    class_send,
    class_recv,
):
    loads = [
        pltpu.make_async_copy(source, target, load_sem.at[i])
        for i, (source, target) in enumerate(
            (
                (tile_hbm, tile_ref),
                (cell_hbm, cell_ref),
                (value_hbm, value_ref),
                (class_hbm, class_ref),
                (coeff_hbm, coeff_ref),
                (lag_hbm, lag_ref),
            )
        )
    ]
    for load in loads[:3]:
        load.start()

    segment = lax.axis_index("year")
    me = lax.axis_index("tile")
    odd = lax.rem(segment, 2)
    near = segment + 1 - 2 * odd
    far = lax.rem(segment + NYEAR - 1 + 2 * odd, NYEAR)

    def day_of(d):
        return d + odd * (DAY_DEV - 1 - 2 * d)

    east = lax.rem(me + 1, NTILE)
    west = lax.rem(me + NTILE - 1, NTILE)
    x, z, y = me // 8, lax.rem(me // 4, 2), lax.rem(me, 4)
    peers = [
        lax.rem(x + dx, 4) * 8 + lax.rem(z + dz, 2) * 4 + lax.rem(y + dy, 4)
        for dx, dz, dy in OFFSETS
    ]

    barrier = pltpu.get_barrier_semaphore()
    for i in reversed(range(1, NTILE)):
        pl.semaphore_signal(barrier, inc=1, device_id={"tile": peers[i]})
    pl.semaphore_signal(barrier, inc=1, device_id={"year": near})
    pl.semaphore_signal(barrier, inc=1, device_id={"year": far})
    for load in loads[3:]:
        load.start()

    for load in loads[:3]:
        load.wait()
    bucket(tile_ref[...], cell_ref[...], value_ref[...], pieces_ref, slots_ref, send_ref)

    pl.semaphore_wait(barrier, NTILE + 1)

    for g, (low, count) in reversed(list(enumerate(GROUPS))):
        for i in reversed(range(max(low, 1), low + count)):
            pltpu.make_async_remote_copy(
                send_ref.at[pl.ds(peers[i], 3)],
                recv_own.at[i],
                list_send,
                list_recv.at[g],
                device_id={"tile": peers[i]},
            ).start()
    recv_own[0] = send_ref[pl.ds(me, 3)]
    loads[3].wait()
    class_t[...] = jnp.transpose(class_ref[...])
    class_copies = [
        pltpu.make_async_remote_copy(
            class_t.at[pl.ds(start, PAD)],
            class_halo.at[1 - side],
            class_send.at[side],
            class_recv.at[1 - side],
            device_id={"tile": tgt},
        )
        for side, start, tgt in ((0, 0, west), (1, LON_DEV - PAD, east))
    ]
    for copy in class_copies:
        copy.start()

    loads[4].wait()
    loads[5].wait()
    mix_ref[...] = jnp.zeros_like(mix_ref)
    for k in range(LAGS):
        hi, lo = split2(lag_ref[k + odd * (LAGS - 1 - 2 * k)])
        for i in range(2):
            lanes = slice((k + i) * LAT, (k + i + 1) * LAT)
            mix_ref[i * LAT : (i + 1) * LAT, lanes] = hi.astype(BF16)
            mix_ref[(2 + i) * LAT : (3 + i) * LAT, lanes] = lo.astype(BF16)

    def coefficients(ids, rows):
        kappa = hzon = hmer = jnp.zeros(ids.shape, F32)
        for c in range(NCLASS):
            here = ids == c
            kappa = jnp.where(here, coeff_ref[0, c], kappa)
            hzon = jnp.where(here, coeff_ref[1, c], hzon)
            hmer = jnp.where(here, coeff_ref[2, c], hmer)
        lane = lax.broadcasted_iota(jnp.int32, ids.shape, 1)
        coef_ref[0, rows] = kappa + 2.0 * hzon + 2.0 * hmer
        coef_ref[1, rows] = hzon
        coef_ref[2, rows] = jnp.where(lane < LAT - 1, hmer, 0.0)
        coef_ref[3, rows] = jnp.where(lane > 0, hmer, 0.0)

    coefficients(class_t[...], slice(PAD, PAD + LON_DEV))

    forwarded = []
    edge_copies = [
        pltpu.make_async_remote_copy(
            edges.at[HALO + i],
            edges.at[HALO - 1 - i],
            edge_send.at[i],
            edge_recv.at[HALO - 1 - i],
            device_id={"year": far},
        )
        for i in range(HALO)
    ]

    def own(group):
        start, count = GROUPS[group]
        low = max(1, start)
        pltpu.make_async_remote_copy(
            recv_own.at[pl.ds(low, start + count - low)],
            recv_own.at[pl.ds(low, start + count - low)],
            list_send,
            list_recv.at[group],
            device_id={"tile": east},
        ).wait_recv()
        copy = pltpu.make_async_remote_copy(
            recv_own.at[pl.ds(start, count), 1],
            recv_far.at[pl.ds(start, count)],
            far_send.at[group],
            far_recv.at[group],
            device_id={"year": far},
        )
        copy.start()
        forwarded.append(copy)
        days = [day_of(d) for d in range(DAY_DEV)]
        scatter_edges(
            recv_own, GROUPS[group], DAY_DEV, day_of, edge_lhs, edge_rhs, edges, HALO
        )
        if group == len(GROUPS) - 1:
            for copy in edge_copies:
                copy.start()
        scatter(recv_own, GROUPS[group], days, lhs_ref, rhs_ref, field, HALO)

    def halo(part):
        senders = FAR_PARTS[part]
        for group, (start, _) in enumerate(GROUPS):
            if senders[0] <= start < sum(senders):
                forwarded[group].wait_recv()
        days = [day_of(d + DAY_DEV - HALO) for d in range(HALO)]
        scatter(recv_far, senders, days, lhs_ref, rhs_ref, field, 0)

    def stencil(src, at, rows):
        v = src[at + (rows,)]
        e = src[at + (slice(rows.start + 1, rows.stop + 1),)]
        w = src[at + (slice(rows.start - 1, rows.stop - 1),)]
        north = pltpu.roll(v, LAT - 1, 1)
        south = pltpu.roll(v, 1, 1)
        return (
            coef_ref[0, rows] * v
            - coef_ref[1, rows] * (e + w)
            - coef_ref[2, rows] * north
            - coef_ref[3, rows] * south
        )

    def keep(e, plane):
        hi, lo = split2(plane)
        smooth_hi[e] = hi.astype(BF16)
        smooth_lo[e] = lo.astype(BF16)

    def smooth(e):
        field[e, PAD - 2 : PAD] = edges[e, :2]
        field[e, PAD + LON_DEV : PAD + LON_DEV + 2] = edges[e, 2:]
        for rows in (
            slice(PAD, PAD + LON_DEV),
            slice(PAD - 1, PAD),
            slice(PAD + LON_DEV, PAD + LON_DEV + 1),
        ):
            once[rows] = stencil(field, (e,), rows)
        twice = stencil(once, (), slice(PAD, PAD + LON_DEV))
        keep(e, twice)
        return twice

    def mix(pair):
        window = range(2 * pair, 2 * pair + LAGS + 1)
        hi = jnp.concatenate([smooth_hi[e] for e in window], axis=1)
        lo = jnp.concatenate([smooth_lo[e] for e in window], axis=1)
        first = dot_nt(mix_ref[...], hi)
        second = dot_nt(mix_ref[: 2 * LAT], lo)
        mixed = first[: 2 * LAT] + (first[2 * LAT :] + second)
        out_ref[day_of(2 * pair)] = mixed[:LAT]
        out_ref[day_of(2 * pair + 1)] = mixed[LAT:]

    for copy in class_copies:
        copy.wait()
    coefficients(class_halo[0], slice(0, PAD))
    coefficients(class_halo[1], slice(PAD + LON_DEV, 2 * PAD + LON_DEV))
    for group in range(len(GROUPS)):
        own(group)
    near_copies = []
    for i, e in enumerate((HALO + DAY_DEV - 1, HALO + DAY_DEV - 2)):
        near_out[i] = smooth(e)
        copy = pltpu.make_async_remote_copy(
            near_out.at[i], near_in.at[i], near_send.at[i], near_recv.at[i], device_id={"year": near}
        )
        copy.start()
        near_copies.append(copy)
    for d in range(DAY_DEV - 2):
        smooth(HALO + d)
    mix(1)
    mix(2)
    for i, copy in enumerate(near_copies):
        copy.wait()
        keep(HALO + DAY_DEV + i, near_in[i])
    mix(3)
    for part in range(len(FAR_PARTS)):
        halo(part)
    for copy in edge_copies:
        copy.wait()
    smooth(1)
    smooth(0)
    mix(0)

    pltpu.make_async_remote_copy(
        recv_own.at[pl.ds(1, NTILE - 1)],
        recv_own.at[pl.ds(1, NTILE - 1)],
        list_send,
        list_recv.at[0],
        device_id={"tile": east},
    ).wait_send()
    for copy in forwarded:
        copy.wait_send()


def body(station_tile, station_cell, station_value, class_ids, coeff_table, lag_blocks):
    hbm = pl.BlockSpec(memory_space=pltpu.HBM)
    dma = pltpu.SemaphoreType.DMA
    groups = len(GROUPS)
    return pl.pallas_call(
        kernel,
        out_shape=pltpu.VMEM((DAY_DEV, LAT, LON_DEV), F32),
        in_specs=[hbm] * 6,
        out_specs=pl.BlockSpec(memory_space=pltpu.VMEM),
        scratch_shapes=[
            pltpu.VMEM((8, LANES), jnp.int32),
            pltpu.VMEM((8, LANES), jnp.int32),
            pltpu.VMEM((8, LANES), F32),
            pltpu.VMEM((LAT, LON_DEV), jnp.int32),
            pltpu.SMEM((3, NCLASS), F32),
            pltpu.VMEM((LAGS, LAT, LAT), F32),
            pltpu.VMEM((5 * NTILE, 8 * LANES), BF16),
            pltpu.VMEM((LANES, 8 * LANES), BF16),
            pltpu.VMEM((NTILE + 2, 2, LANES), F32),
            pltpu.VMEM((NTILE, 3, 2, LANES), F32),
            pltpu.VMEM((NTILE, 2, LANES), F32),
            pltpu.VMEM((LON_DEV, LAT), jnp.int32),
            pltpu.VMEM((2, PAD, LAT), jnp.int32),
            pltpu.VMEM((4, LON_DEV + 2 * PAD, LAT), F32),
            pltpu.VMEM((2 * LON_DEV, MOST * CAP), BF16),
            pltpu.VMEM((DAY_DEV * LAT, MOST * CAP), BF16),
            pltpu.VMEM((8 * DAY_DEV, 2 * MOST * CAP), BF16),
            pltpu.VMEM((LAT, 2 * MOST * CAP), BF16),
            pltpu.VMEM((DAYS_EXT, LON_DEV + 2 * PAD, LAT), F32),
            pltpu.VMEM((DAYS_EXT, 4, LAT), F32),
            pltpu.VMEM((LON_DEV + 2 * PAD, LAT), F32),
            pltpu.VMEM((4 * LAT, (LAGS + 1) * LAT), BF16),
            pltpu.VMEM((DAYS_EXT, LON_DEV, LAT), BF16),
            pltpu.VMEM((DAYS_EXT, LON_DEV, LAT), BF16),
            pltpu.VMEM((HALO, LON_DEV, LAT), F32),
            pltpu.VMEM((HALO, LON_DEV, LAT), F32),
            dma((6,)),
            dma,
            dma((groups,)),
            dma((groups,)),
            dma((groups,)),
            dma((HALO,)),
            dma((HALO,)),
            dma((HALO,)),
            dma((HALO,)),
            dma((2,)),
            dma((2,)),
        ],
        compiler_params=pltpu.CompilerParams(
            collective_id=0, has_side_effects=True, vmem_limit_bytes=40 * 2**20
        ),
    )(
        *(
            pltpu.with_memory_space_constraint(x, pltpu.HBM)
            for x in (
                station_tile.reshape(8, LANES),
                station_cell.reshape(8, LANES),
                station_value.reshape(8, LANES),
                class_ids,
                coeff_table,
                lag_blocks,
            )
        )
    )


def solution(mesh):
    in_specs = (
        P(("year", "tile"), None),
        P(("year", "tile")),
        P(("year", "tile")),
        P(None, "tile"),
        P(),
        P(),
    )
    out_specs = P("year", None, "tile")
    return jax.shard_map(body, mesh=mesh, in_specs=in_specs, out_specs=out_specs, check_vma=False)
```

```python
import jax
import jax.numpy as jnp
from jax import lax
from jax.experimental import pallas as pl
from jax.experimental.pallas import tpu as pltpu
from jax.sharding import PartitionSpec as P

DAY_DEV = 8
LAT = 128
LON_DEV = 256
CAP = 96
LANES = 128
NTILE = 32
NYEAR = 4
NCLASS = 16
GROUPS = ((0, 32),)
MOST = 32
LAGS = 5
HALO = 2
DAYS_EXT = DAY_DEV + 2 * HALO
PAD = 8
F32 = jnp.float32
BF16 = jnp.bfloat16


def dot_nt(a, b):
    return lax.dot_general(a, b, (((1,), (1,)), ((), ())), preferred_element_type=F32)


def split2(x):
    hi = x.astype(BF16).astype(F32)
    return hi, x - hi


def hot(mask):
    return jnp.where(mask, 1.0, 0.0).astype(BF16)


def hops(offset):
    return sum(min(o, n - o) * step for o, n, step in zip(offset, (4, 2, 4), (1, 2, 1)))


OFFSETS = sorted(((x, z, y) for x in range(4) for z in range(2) for y in range(4)), key=hops)


def spread(row, count):
    few = jnp.broadcast_to(row.astype(F32), (16, LANES)).astype(BF16)
    return jnp.concatenate([few] * (count // 16), axis=0)


def numbers(count):
    return lax.broadcasted_iota(jnp.int32, (count, LANES), 0).astype(F32).astype(BF16)


def pick(row, iota, piece=None):
    count = iota.shape[0]
    value = jnp.ones((), BF16) if piece is None else spread(piece, count)
    return jnp.where(spread(row, count) == iota, value, jnp.zeros((), BF16))


def bucket(tile, cell, value, pieces_ref, slots_ref, send_ref):
    hi, mid = split2(value)
    day = jnp.right_shift(cell, 15).astype(F32)
    row = jnp.bitwise_and(jnp.right_shift(cell, 8), 127).astype(F32)
    col = jnp.bitwise_and(cell, 255).astype(F32)
    of_tile = lax.broadcasted_iota(jnp.int32, (NTILE, LANES), 0)
    masks = [tile[b : b + 1, :] == of_tile for b in range(8)]
    ones = jnp.concatenate([hot(m) for m in masks], axis=0)
    source = lax.broadcasted_iota(jnp.int32, (LANES, 2 * LANES), 0)
    target = lax.broadcasted_iota(jnp.int32, (LANES, 2 * LANES), 1)
    before = hot((source < target) | (target >= LANES))
    counts = jnp.dot(ones, before, preferred_element_type=F32)
    base = jnp.zeros((NTILE, LANES), F32)
    slot_iota = lax.broadcasted_iota(jnp.int32, (LANES, LANES), 0).astype(F32)
    for b in range(8):
        lanes = slice(b * LANES, (b + 1) * LANES)
        rank = counts[b * NTILE : (b + 1) * NTILE, :LANES] + base
        base = base + counts[b * NTILE : (b + 1) * NTILE, LANES:]
        slot = jnp.sum(jnp.where(masks[b], rank, 0.0), axis=0, keepdims=True)
        slots_ref[:, lanes] = hot(slot_iota == slot)
        for q, piece in enumerate((hi, mid, day, row, col)):
            pieces_ref[q * NTILE : (q + 1) * NTILE, lanes] = jnp.where(
                masks[b], piece[b : b + 1, :], 0.0
            ).astype(BF16)
    out = dot_nt(pieces_ref[...], slots_ref[...])
    part = [out[q * NTILE : (q + 1) * NTILE] for q in range(5)]
    values = part[0] + part[1]
    cells = part[2] * 32768.0 + part[3] * 256.0 + part[4]
    for q, x in enumerate((values, cells)):
        send_ref[1 : NTILE + 1, q, :] = x
        send_ref[0:1, q, :] = x[NTILE - 1 :]
        send_ref[NTILE + 1 : NTILE + 2, q, :] = x[:1]


def dense(lists):
    lane = lax.broadcasted_iota(jnp.int32, (1, LANES), 1)
    turned = [pltpu.roll(lists, shift, 1) for shift in (96, 64, 32)]
    return [
        jnp.where(lane < CAP, lists[i + j : i + j + 1], turned[j][i + 3 : i + 4])
        for i in range(0, lists.shape[0], 4)
        for j in range(3)
    ]


def entries(recv_ref, senders, which):
    at = slice(senders[0], sum(senders))
    if len(recv_ref.shape) == 3:
        value, cell = recv_ref[at, 0, :], recv_ref[at, 1, :]
    else:
        value, cell = recv_ref[at, which, 0, :], recv_ref[at, which, 1, :]
    hi, lo = split2(value)
    return hi, lo, cell.astype(jnp.int32)


def scatter(recv_ref, senders, days, lhs_ref, rhs_ref, field, first):
    hi, lo, cell = entries(recv_ref, senders, 1)
    hi, lo = dense(hi), dense(lo)
    col = dense(jnp.bitwise_and(cell, 255))
    plane = dense(jnp.right_shift(cell, 8))
    depth = len(col) * LANES
    column, latitude = numbers(LON_DEV), numbers(LAT)
    for k in range(len(col)):
        lanes = slice(k * LANES, (k + 1) * LANES)
        lhs_ref[:LON_DEV, lanes] = pick(col[k], column, hi[k])
        lhs_ref[LON_DEV:, lanes] = pick(col[k], column, lo[k])
    for i, d in enumerate(days):
        for k in range(len(col)):
            rhs_ref[i * LAT : (i + 1) * LAT, k * LANES : (k + 1) * LANES] = pick(
                plane[k] - d * LAT, latitude
            )
    for pair in range(len(days) // 2):
        both = dot_nt(
            lhs_ref[:, :depth], rhs_ref[2 * LAT * pair : 2 * LAT * (pair + 1), :depth]
        )
        both = both[:LON_DEV] + both[LON_DEV:]
        for i in range(2):
            part = both[:, i * LAT : (i + 1) * LAT]
            e = first + 2 * pair + i
            if senders[0] == 0:
                field[e, PAD : PAD + LON_DEV] = part
            else:
                field[e, PAD : PAD + LON_DEV] += part


def scatter_edges(recv_ref, senders, count, number_of, lhs_ref, rhs_ref, edges, first):
    rows = 4 * count
    padded = max(rows, 16)
    latitude, number = numbers(LAT), numbers(padded)
    blocks = 3 * senders[1] // 4
    for j, which in enumerate((0, 2)):
        hi, lo, cell = entries(recv_ref, senders, which)
        col = jnp.bitwise_and(cell, 255)
        near = col >= LON_DEV - 2 if which == 0 else col < 2
        place = 4 * number_of(jnp.right_shift(cell, 15)) + (
            col - (LON_DEV - 2) if which == 0 else col + 2
        )
        place = dense(jnp.where(near, place, -1))
        lat = dense(jnp.bitwise_and(jnp.right_shift(cell, 8), LAT - 1))
        hi, lo = dense(hi), dense(lo)
        for k in range(blocks):
            lanes = slice((blocks * j + k) * LANES, (blocks * j + k + 1) * LANES)
            lhs_ref[:padded, lanes] = pick(place[k], number, hi[k])
            lhs_ref[padded : 2 * padded, lanes] = pick(place[k], number, lo[k])
            rhs_ref[:, lanes] = pick(lat[k], latitude)
    depth = 2 * blocks * LANES
    both = dot_nt(lhs_ref[: 2 * padded, :depth], rhs_ref[:, :depth])
    both = both[:padded] + both[padded:]
    for i in range(count):
        if senders[0] == 0:
            edges[first + i] = both[4 * i : 4 * i + 4]
        else:
            edges[first + i] += both[4 * i : 4 * i + 4]


def kernel(
    tile_hbm,
    cell_hbm,
    value_hbm,
    class_hbm,
    coeff_hbm,
    lag_hbm,
    out_ref,
    tile_ref,
    cell_ref,
    value_ref,
    class_ref,
    coeff_ref,
    lag_ref,
    pieces_ref,
    slots_ref,
    send_ref,
    recv_own,
    recv_far,
    class_t,
    class_halo,
    coef_ref,
    lhs_ref,
    rhs_ref,
    edge_lhs,
    edge_rhs,
    field,
    edges,
    once,
    mix_ref,
    smooth_hi,
    smooth_lo,
    near_out,
    near_in,
    load_sem,
    list_send,
    list_recv,
    far_send,
    far_recv,
    near_send,
    near_recv,
    edge_send,
    edge_recv,
    class_send,
    class_recv,
):
    loads = [
        pltpu.make_async_copy(source, target, load_sem.at[i])
        for i, (source, target) in enumerate(
            (
                (tile_hbm, tile_ref),
                (cell_hbm, cell_ref),
                (value_hbm, value_ref),
                (class_hbm, class_ref),
                (coeff_hbm, coeff_ref),
                (lag_hbm, lag_ref),
            )
        )
    ]
    for load in loads[:3]:
        load.start()

    segment = lax.axis_index("year")
    me = lax.axis_index("tile")
    odd = lax.rem(segment, 2)
    near = segment + 1 - 2 * odd
    far = lax.rem(segment + NYEAR - 1 + 2 * odd, NYEAR)

    def day_of(d):
        return d + odd * (DAY_DEV - 1 - 2 * d)

    east = lax.rem(me + 1, NTILE)
    west = lax.rem(me + NTILE - 1, NTILE)
    x, z, y = me // 8, lax.rem(me // 4, 2), lax.rem(me, 4)
    peers = [
        lax.rem(x + dx, 4) * 8 + lax.rem(z + dz, 2) * 4 + lax.rem(y + dy, 4)
        for dx, dz, dy in OFFSETS
    ]

    barrier = pltpu.get_barrier_semaphore()
    for i in reversed(range(1, NTILE)):
        pl.semaphore_signal(barrier, inc=1, device_id={"tile": peers[i]})
    pl.semaphore_signal(barrier, inc=1, device_id={"year": near})
    pl.semaphore_signal(barrier, inc=1, device_id={"year": far})
    for load in loads[3:]:
        load.start()

    for load in loads[:3]:
        load.wait()
    bucket(tile_ref[...], cell_ref[...], value_ref[...], pieces_ref, slots_ref, send_ref)

    pl.semaphore_wait(barrier, NTILE + 1)

    for g, (low, count) in reversed(list(enumerate(GROUPS))):
        for i in reversed(range(max(low, 1), low + count)):
            pltpu.make_async_remote_copy(
                send_ref.at[pl.ds(peers[i], 3)],
                recv_own.at[i],
                list_send,
                list_recv.at[g],
                device_id={"tile": peers[i]},
            ).start()
    recv_own[0] = send_ref[pl.ds(me, 3)]
    loads[3].wait()
    class_t[...] = jnp.transpose(class_ref[...])
    class_copies = [
        pltpu.make_async_remote_copy(
            class_t.at[pl.ds(start, PAD)],
            class_halo.at[1 - side],
            class_send.at[side],
            class_recv.at[1 - side],
            device_id={"tile": tgt},
        )
        for side, start, tgt in ((0, 0, west), (1, LON_DEV - PAD, east))
    ]
    for copy in class_copies:
        copy.start()

    loads[4].wait()
    loads[5].wait()
    mix_ref[...] = jnp.zeros_like(mix_ref)
    for k in range(LAGS):
        hi, lo = split2(lag_ref[k + odd * (LAGS - 1 - 2 * k)])
        for i in range(2):
            lanes = slice((k + i) * LAT, (k + i + 1) * LAT)
            mix_ref[i * LAT : (i + 1) * LAT, lanes] = hi.astype(BF16)
            mix_ref[(2 + i) * LAT : (3 + i) * LAT, lanes] = lo.astype(BF16)

    def coefficients(ids, rows):
        kappa = hzon = hmer = jnp.zeros(ids.shape, F32)
        for c in range(NCLASS):
            here = ids == c
            kappa = jnp.where(here, coeff_ref[0, c], kappa)
            hzon = jnp.where(here, coeff_ref[1, c], hzon)
            hmer = jnp.where(here, coeff_ref[2, c], hmer)
        lane = lax.broadcasted_iota(jnp.int32, ids.shape, 1)
        coef_ref[0, rows] = kappa + 2.0 * hzon + 2.0 * hmer
        coef_ref[1, rows] = hzon
        coef_ref[2, rows] = jnp.where(lane < LAT - 1, hmer, 0.0)
        coef_ref[3, rows] = jnp.where(lane > 0, hmer, 0.0)

    coefficients(class_t[...], slice(PAD, PAD + LON_DEV))

    def section(f):
        pl.when(me < NTILE)(f)

    forwarded = []
    edge_copies = [
        pltpu.make_async_remote_copy(
            edges.at[HALO + i],
            edges.at[HALO - 1 - i],
            edge_send.at[i],
            edge_recv.at[HALO - 1 - i],
            device_id={"year": far},
        )
        for i in range(HALO)
    ]

    def own(group):
        start, count = GROUPS[group]
        low = max(1, start)
        pltpu.make_async_remote_copy(
            recv_own.at[pl.ds(low, start + count - low)],
            recv_own.at[pl.ds(low, start + count - low)],
            list_send,
            list_recv.at[group],
            device_id={"tile": east},
        ).wait_recv()
        copy = pltpu.make_async_remote_copy(
            recv_own.at[pl.ds(start, count), 1],
            recv_far.at[pl.ds(start, count)],
            far_send.at[group],
            far_recv.at[group],
            device_id={"year": far},
        )
        copy.start()
        forwarded.append(copy)
        days = [day_of(d) for d in range(DAY_DEV)]

        @section
        def _():
            scatter_edges(
                recv_own, GROUPS[group], DAY_DEV, day_of, edge_lhs, edge_rhs, edges, HALO
            )

        if group == len(GROUPS) - 1:
            for copy in edge_copies:
                copy.start()

        @section
        def _():
            scatter(recv_own, GROUPS[group], days, lhs_ref, rhs_ref, field, HALO)
            if group == len(GROUPS) - 1:
                for i, e in enumerate((HALO + DAY_DEV - 1, HALO + DAY_DEV - 2)):
                    near_out[i] = smooth(e)

    def scatter_far():
        days = [day_of(d + DAY_DEV - HALO) for d in range(HALO)]
        scatter(recv_far, (0, NTILE), days, lhs_ref, rhs_ref, field, 0)

    def stencil(src, at, rows):
        v = src[at + (rows,)]
        e = src[at + (slice(rows.start + 1, rows.stop + 1),)]
        w = src[at + (slice(rows.start - 1, rows.stop - 1),)]
        north = pltpu.roll(v, LAT - 1, 1)
        south = pltpu.roll(v, 1, 1)
        return (
            coef_ref[0, rows] * v
            - coef_ref[1, rows] * (e + w)
            - coef_ref[2, rows] * north
            - coef_ref[3, rows] * south
        )

    def keep(e, plane):
        hi, lo = split2(plane)
        smooth_hi[e] = hi.astype(BF16)
        smooth_lo[e] = lo.astype(BF16)

    def smooth(e):
        field[e, PAD - 2 : PAD] = edges[e, :2]
        field[e, PAD + LON_DEV : PAD + LON_DEV + 2] = edges[e, 2:]
        for rows in (
            slice(PAD, PAD + LON_DEV),
            slice(PAD - 1, PAD),
            slice(PAD + LON_DEV, PAD + LON_DEV + 1),
        ):
            once[rows] = stencil(field, (e,), rows)
        twice = stencil(once, (), slice(PAD, PAD + LON_DEV))
        keep(e, twice)
        return twice

    def mix(pair):
        window = range(2 * pair, 2 * pair + LAGS + 1)
        hi = jnp.concatenate([smooth_hi[e] for e in window], axis=1)
        lo = jnp.concatenate([smooth_lo[e] for e in window], axis=1)
        first = dot_nt(mix_ref[...], hi)
        second = dot_nt(mix_ref[: 2 * LAT], lo)
        mixed = first[: 2 * LAT] + (first[2 * LAT :] + second)
        out_ref[day_of(2 * pair)] = mixed[:LAT]
        out_ref[day_of(2 * pair + 1)] = mixed[LAT:]

    for copy in class_copies:
        copy.wait()
    coefficients(class_halo[0], slice(0, PAD))
    coefficients(class_halo[1], slice(PAD + LON_DEV, 2 * PAD + LON_DEV))
    for group in range(len(GROUPS)):
        own(group)
    near_copies = []
    for i, e in enumerate((HALO + DAY_DEV - 1, HALO + DAY_DEV - 2)):
        copy = pltpu.make_async_remote_copy(
            near_out.at[i], near_in.at[i], near_send.at[i], near_recv.at[i], device_id={"year": near}
        )
        copy.start()
        near_copies.append(copy)

    for copy in forwarded:
        copy.wait_recv()

    @section
    def _():
        scatter_far()
        for d in range(DAY_DEV - 2):
            smooth(HALO + d)
        mix(1)
        mix(2)

    for copy in near_copies + edge_copies:
        copy.wait()
    for i in range(HALO):
        keep(HALO + DAY_DEV + i, near_in[i])
    mix(3)
    smooth(1)
    smooth(0)
    mix(0)

    pltpu.make_async_remote_copy(
        recv_own.at[pl.ds(1, NTILE - 1)],
        recv_own.at[pl.ds(1, NTILE - 1)],
        list_send,
        list_recv.at[0],
        device_id={"tile": east},
    ).wait_send()
    for copy in forwarded:
        copy.wait_send()


def body(station_tile, station_cell, station_value, class_ids, coeff_table, lag_blocks):
    hbm = pl.BlockSpec(memory_space=pltpu.HBM)
    dma = pltpu.SemaphoreType.DMA
    groups = len(GROUPS)
    return pl.pallas_call(
        kernel,
        out_shape=pltpu.VMEM((DAY_DEV, LAT, LON_DEV), F32),
        in_specs=[hbm] * 6,
        out_specs=pl.BlockSpec(memory_space=pltpu.VMEM),
        scratch_shapes=[
            pltpu.VMEM((8, LANES), jnp.int32),
            pltpu.VMEM((8, LANES), jnp.int32),
            pltpu.VMEM((8, LANES), F32),
            pltpu.VMEM((LAT, LON_DEV), jnp.int32),
            pltpu.SMEM((3, NCLASS), F32),
            pltpu.VMEM((LAGS, LAT, LAT), F32),
            pltpu.VMEM((5 * NTILE, 8 * LANES), BF16),
            pltpu.VMEM((LANES, 8 * LANES), BF16),
            pltpu.VMEM((NTILE + 2, 2, LANES), F32),
            pltpu.VMEM((NTILE, 3, 2, LANES), F32),
            pltpu.VMEM((NTILE, 2, LANES), F32),
            pltpu.VMEM((LON_DEV, LAT), jnp.int32),
            pltpu.VMEM((2, PAD, LAT), jnp.int32),
            pltpu.VMEM((4, LON_DEV + 2 * PAD, LAT), F32),
            pltpu.VMEM((2 * LON_DEV, MOST * CAP), BF16),
            pltpu.VMEM((DAY_DEV * LAT, MOST * CAP), BF16),
            pltpu.VMEM((8 * DAY_DEV, 2 * MOST * CAP), BF16),
            pltpu.VMEM((LAT, 2 * MOST * CAP), BF16),
            pltpu.VMEM((DAYS_EXT, LON_DEV + 2 * PAD, LAT), F32),
            pltpu.VMEM((DAYS_EXT, 4, LAT), F32),
            pltpu.VMEM((LON_DEV + 2 * PAD, LAT), F32),
            pltpu.VMEM((4 * LAT, (LAGS + 1) * LAT), BF16),
            pltpu.VMEM((DAYS_EXT, LON_DEV, LAT), BF16),
            pltpu.VMEM((DAYS_EXT, LON_DEV, LAT), BF16),
            pltpu.VMEM((HALO, LON_DEV, LAT), F32),
            pltpu.VMEM((HALO, LON_DEV, LAT), F32),
            dma((6,)),
            dma,
            dma((groups,)),
            dma((groups,)),
            dma((groups,)),
            dma((HALO,)),
            dma((HALO,)),
            dma((HALO,)),
            dma((HALO,)),
            dma((2,)),
            dma((2,)),
        ],
        compiler_params=pltpu.CompilerParams(
            collective_id=0, has_side_effects=True, vmem_limit_bytes=40 * 2**20
        ),
    )(
        *(
            pltpu.with_memory_space_constraint(x, pltpu.HBM)
            for x in (
                station_tile.reshape(8, LANES),
                station_cell.reshape(8, LANES),
                station_value.reshape(8, LANES),
                class_ids,
                coeff_table,
                lag_blocks,
            )
        )
    )


def solution(mesh):
    in_specs = (
        P(("year", "tile"), None),
        P(("year", "tile")),
        P(("year", "tile")),
        P(None, "tile"),
        P(),
        P(),
    )
    out_specs = P("year", None, "tile")
    return jax.shard_map(body, mesh=mesh, in_specs=in_specs, out_specs=out_specs, check_vma=False)
```

```python
import jax
import jax.numpy as jnp
from jax import lax
from jax.experimental import pallas as pl
from jax.experimental.pallas import tpu as pltpu
from jax.sharding import PartitionSpec as P

DAY_DEV = 8
LAT = 128
LON_DEV = 256
CAP = 96
LANES = 128
NTILE = 32
NYEAR = 4
NCLASS = 16
GROUPS = ((0, 32),)
MOST = 32
LAGS = 5
HALO = 2
DAYS_EXT = DAY_DEV + 2 * HALO
PAD = 8
F32 = jnp.float32
BF16 = jnp.bfloat16
F8 = jnp.float8_e4m3fn


def dot_nt(a, b):
    return lax.dot_general(a, b, (((1,), (1,)), ((), ())), preferred_element_type=F32)


def split2(x):
    hi = x.astype(BF16).astype(F32)
    return hi, x - hi


def hot(mask):
    return jnp.where(mask, 1.0, 0.0).astype(BF16)


def hops(offset):
    return sum(min(o, n - o) * step for o, n, step in zip(offset, (4, 2, 4), (1, 2, 1)))


OFFSETS = sorted(((x, z, y) for x in range(4) for z in range(2) for y in range(4)), key=hops)


def spread(row, count):
    few = jnp.broadcast_to(row.astype(F32), (16, LANES)).astype(BF16)
    return jnp.concatenate([few] * (count // 16), axis=0)


def numbers(count):
    return lax.broadcasted_iota(jnp.int32, (count, LANES), 0).astype(F32).astype(BF16)


def pick(row, iota, piece=None):
    count = iota.shape[0]
    value = jnp.ones((), BF16) if piece is None else spread(piece, count)
    return jnp.where(spread(row, count) == iota, value, jnp.zeros((), BF16))


def bucket(tile, cell, value, pieces_ref, slots_ref, send_ref):
    hi, mid = split2(value)
    day = jnp.right_shift(cell, 15).astype(F32)
    row = jnp.bitwise_and(jnp.right_shift(cell, 8), 127).astype(F32)
    col = jnp.bitwise_and(cell, 255).astype(F32)
    of_tile = lax.broadcasted_iota(jnp.int32, (NTILE, LANES), 0)
    masks = [tile[b : b + 1, :] == of_tile for b in range(8)]
    ones = jnp.concatenate([hot(m) for m in masks], axis=0)
    source = lax.broadcasted_iota(jnp.int32, (LANES, 2 * LANES), 0)
    target = lax.broadcasted_iota(jnp.int32, (LANES, 2 * LANES), 1)
    before = hot((source < target) | (target >= LANES))
    counts = jnp.dot(ones, before, preferred_element_type=F32)
    base = jnp.zeros((NTILE, LANES), F32)
    slot_iota = lax.broadcasted_iota(jnp.int32, (LANES, LANES), 0).astype(F32)
    for b in range(8):
        lanes = slice(b * LANES, (b + 1) * LANES)
        rank = counts[b * NTILE : (b + 1) * NTILE, :LANES] + base
        base = base + counts[b * NTILE : (b + 1) * NTILE, LANES:]
        slot = jnp.sum(jnp.where(masks[b], rank, 0.0), axis=0, keepdims=True)
        slots_ref[:, lanes] = hot(slot_iota == slot)
        for q, piece in enumerate((hi, mid, day, row, col)):
            pieces_ref[q * NTILE : (q + 1) * NTILE, lanes] = jnp.where(
                masks[b], piece[b : b + 1, :], 0.0
            ).astype(BF16)
    out = dot_nt(pieces_ref[...], slots_ref[...])
    part = [out[q * NTILE : (q + 1) * NTILE] for q in range(5)]
    values = part[0] + part[1]
    cells = part[2] * 32768.0 + part[3] * 256.0 + part[4]
    for q, x in enumerate((values, cells)):
        send_ref[1 : NTILE + 1, q, :] = x
        send_ref[0:1, q, :] = x[NTILE - 1 :]
        send_ref[NTILE + 1 : NTILE + 2, q, :] = x[:1]


def dense(lists):
    lane = lax.broadcasted_iota(jnp.int32, (1, LANES), 1)
    turned = [pltpu.roll(lists, shift, 1) for shift in (96, 64, 32)]
    return [
        jnp.where(lane < CAP, lists[i + j : i + j + 1], turned[j][i + 3 : i + 4])
        for i in range(0, lists.shape[0], 4)
        for j in range(3)
    ]


def entries(recv_ref, senders, which):
    at = slice(senders[0], sum(senders))
    if len(recv_ref.shape) == 3:
        value, cell = recv_ref[at, 0, :], recv_ref[at, 1, :]
    else:
        value, cell = recv_ref[at, which, 0, :], recv_ref[at, which, 1, :]
    hi, lo = split2(value)
    return hi, lo, cell.astype(jnp.int32)


def scatter(recv_ref, senders, days, lhs_ref, rhs_ref, field, first):
    hi, lo, cell = entries(recv_ref, senders, 1)
    largest = jnp.maximum(jnp.max(jnp.abs(hi + lo), axis=(0, 1), keepdims=True), 1e-35)
    rest = (hi + lo) * (256.0 / largest)
    pieces = []
    for _ in range(3):
        piece = rest.astype(F8).astype(F32)
        rest = (rest - piece) * 16.0
        pieces.append(dense(piece))
    col = dense(jnp.bitwise_and(cell, 255))
    plane = dense(jnp.right_shift(cell, 8))
    depth = len(col) * LANES
    column, latitude = numbers(LON_DEV), numbers(LAT)
    for k in range(len(col)):
        lanes = slice(k * LANES, (k + 1) * LANES)
        for q, piece in enumerate(pieces):
            lhs_ref[q * LON_DEV : (q + 1) * LON_DEV, lanes] = pick(col[k], column, piece[k]).astype(F8)
    for i, d in enumerate(days):
        for k in range(len(col)):
            rhs_ref[i * LAT : (i + 1) * LAT, k * LANES : (k + 1) * LANES] = pick(
                plane[k] - d * LAT, latitude
            ).astype(F8)
    for pair in range(len(days) // 2):
        both = dot_nt(
            lhs_ref[:, :depth], rhs_ref[2 * LAT * pair : 2 * LAT * (pair + 1), :depth]
        )
        small = both[LON_DEV : 2 * LON_DEV] + both[2 * LON_DEV :] * (1.0 / 16.0)
        both = (both[:LON_DEV] + small * (1.0 / 16.0)) * (largest * (1.0 / 256.0))
        for i in range(2):
            part = both[:, i * LAT : (i + 1) * LAT]
            e = first + 2 * pair + i
            if senders[0] == 0:
                field[e, PAD : PAD + LON_DEV] = part
            else:
                field[e, PAD : PAD + LON_DEV] += part


def scatter_edges(recv_ref, senders, count, number_of, lhs_ref, rhs_ref, edges, first):
    rows = 4 * count
    padded = max(rows, 16)
    latitude, number = numbers(LAT), numbers(padded)
    blocks = 3 * senders[1] // 4
    for j, which in enumerate((0, 2)):
        hi, lo, cell = entries(recv_ref, senders, which)
        col = jnp.bitwise_and(cell, 255)
        near = col >= LON_DEV - 2 if which == 0 else col < 2
        place = 4 * number_of(jnp.right_shift(cell, 15)) + (
            col - (LON_DEV - 2) if which == 0 else col + 2
        )
        place = dense(jnp.where(near, place, -1))
        lat = dense(jnp.bitwise_and(jnp.right_shift(cell, 8), LAT - 1))
        hi, lo = dense(hi), dense(lo)
        for k in range(blocks):
            lanes = slice((blocks * j + k) * LANES, (blocks * j + k + 1) * LANES)
            lhs_ref[:padded, lanes] = pick(place[k], number, hi[k])
            lhs_ref[padded : 2 * padded, lanes] = pick(place[k], number, lo[k])
            rhs_ref[:, lanes] = pick(lat[k], latitude)
    depth = 2 * blocks * LANES
    both = dot_nt(lhs_ref[: 2 * padded, :depth], rhs_ref[:, :depth])
    both = both[:padded] + both[padded:]
    for i in range(count):
        if senders[0] == 0:
            edges[first + i] = both[4 * i : 4 * i + 4]
        else:
            edges[first + i] += both[4 * i : 4 * i + 4]


def kernel(
    tile_hbm,
    cell_hbm,
    value_hbm,
    class_hbm,
    coeff_hbm,
    lag_hbm,
    out_ref,
    tile_ref,
    cell_ref,
    value_ref,
    class_ref,
    coeff_ref,
    lag_ref,
    pieces_ref,
    slots_ref,
    send_ref,
    recv_own,
    recv_far,
    class_t,
    class_halo,
    coef_ref,
    lhs_ref,
    rhs_ref,
    edge_lhs,
    edge_rhs,
    field,
    edges,
    once,
    mix_ref,
    smooth_hi,
    smooth_lo,
    near_out,
    near_in,
    load_sem,
    list_send,
    list_recv,
    far_send,
    far_recv,
    near_send,
    near_recv,
    edge_send,
    edge_recv,
    class_send,
    class_recv,
):
    loads = [
        pltpu.make_async_copy(source, target, load_sem.at[i])
        for i, (source, target) in enumerate(
            (
                (tile_hbm, tile_ref),
                (cell_hbm, cell_ref),
                (value_hbm, value_ref),
                (class_hbm, class_ref),
                (coeff_hbm, coeff_ref),
                (lag_hbm, lag_ref),
            )
        )
    ]
    for load in loads[:3]:
        load.start()

    segment = lax.axis_index("year")
    me = lax.axis_index("tile")
    odd = lax.rem(segment, 2)
    near = segment + 1 - 2 * odd
    far = lax.rem(segment + NYEAR - 1 + 2 * odd, NYEAR)

    def day_of(d):
        return d + odd * (DAY_DEV - 1 - 2 * d)

    east = lax.rem(me + 1, NTILE)
    west = lax.rem(me + NTILE - 1, NTILE)
    x, z, y = me // 8, lax.rem(me // 4, 2), lax.rem(me, 4)
    peers = [
        lax.rem(x + dx, 4) * 8 + lax.rem(z + dz, 2) * 4 + lax.rem(y + dy, 4)
        for dx, dz, dy in OFFSETS
    ]

    barrier = pltpu.get_barrier_semaphore()
    for i in reversed(range(1, NTILE)):
        pl.semaphore_signal(barrier, inc=1, device_id={"tile": peers[i]})
    pl.semaphore_signal(barrier, inc=1, device_id={"year": near})
    pl.semaphore_signal(barrier, inc=1, device_id={"year": far})
    for load in loads[3:]:
        load.start()

    for load in loads[:3]:
        load.wait()
    bucket(tile_ref[...], cell_ref[...], value_ref[...], pieces_ref, slots_ref, send_ref)

    pl.semaphore_wait(barrier, NTILE + 1)

    for g, (low, count) in reversed(list(enumerate(GROUPS))):
        for i in reversed(range(max(low, 1), low + count)):
            pltpu.make_async_remote_copy(
                send_ref.at[pl.ds(peers[i], 3)],
                recv_own.at[i],
                list_send,
                list_recv.at[g],
                device_id={"tile": peers[i]},
            ).start()
    recv_own[0] = send_ref[pl.ds(me, 3)]
    loads[3].wait()
    class_t[...] = jnp.transpose(class_ref[...])
    class_copies = [
        pltpu.make_async_remote_copy(
            class_t.at[pl.ds(start, PAD)],
            class_halo.at[1 - side],
            class_send.at[side],
            class_recv.at[1 - side],
            device_id={"tile": tgt},
        )
        for side, start, tgt in ((0, 0, west), (1, LON_DEV - PAD, east))
    ]
    for copy in class_copies:
        copy.start()

    loads[4].wait()
    loads[5].wait()
    mix_ref[...] = jnp.zeros_like(mix_ref)
    for k in range(LAGS):
        hi, lo = split2(lag_ref[k + odd * (LAGS - 1 - 2 * k)])
        for i in range(2):
            lanes = slice((k + i) * LAT, (k + i + 1) * LAT)
            mix_ref[i * LAT : (i + 1) * LAT, lanes] = hi.astype(BF16)
            mix_ref[(2 + i) * LAT : (3 + i) * LAT, lanes] = lo.astype(BF16)

    def coefficients(ids, rows):
        kappa = hzon = hmer = jnp.zeros(ids.shape, F32)
        for c in range(NCLASS):
            here = ids == c
            kappa = jnp.where(here, coeff_ref[0, c], kappa)
            hzon = jnp.where(here, coeff_ref[1, c], hzon)
            hmer = jnp.where(here, coeff_ref[2, c], hmer)
        lane = lax.broadcasted_iota(jnp.int32, ids.shape, 1)
        coef_ref[0, rows] = kappa + 2.0 * hzon + 2.0 * hmer
        coef_ref[1, rows] = hzon
        coef_ref[2, rows] = jnp.where(lane < LAT - 1, hmer, 0.0)
        coef_ref[3, rows] = jnp.where(lane > 0, hmer, 0.0)

    coefficients(class_t[...], slice(PAD, PAD + LON_DEV))

    def section(f):
        pl.when(me < NTILE)(f)

    forwarded = []
    edge_copies = [
        pltpu.make_async_remote_copy(
            edges.at[HALO + i],
            edges.at[HALO - 1 - i],
            edge_send.at[i],
            edge_recv.at[HALO - 1 - i],
            device_id={"year": far},
        )
        for i in range(HALO)
    ]

    def own(group):
        start, count = GROUPS[group]
        low = max(1, start)
        pltpu.make_async_remote_copy(
            recv_own.at[pl.ds(low, start + count - low)],
            recv_own.at[pl.ds(low, start + count - low)],
            list_send,
            list_recv.at[group],
            device_id={"tile": east},
        ).wait_recv()
        copy = pltpu.make_async_remote_copy(
            recv_own.at[pl.ds(start, count), 1],
            recv_far.at[pl.ds(start, count)],
            far_send.at[group],
            far_recv.at[group],
            device_id={"year": far},
        )
        copy.start()
        forwarded.append(copy)
        days = [day_of(d) for d in range(DAY_DEV)]

        @section
        def _():
            scatter_edges(
                recv_own, GROUPS[group], DAY_DEV, day_of, edge_lhs, edge_rhs, edges, HALO
            )

        if group == len(GROUPS) - 1:
            for copy in edge_copies:
                copy.start()

        @section
        def _():
            scatter(recv_own, GROUPS[group], days, lhs_ref, rhs_ref, field, HALO)
            if group == len(GROUPS) - 1:
                for i, e in enumerate((HALO + DAY_DEV - 1, HALO + DAY_DEV - 2)):
                    near_out[i] = smooth(e)

    def scatter_far():
        days = [day_of(d + DAY_DEV - HALO) for d in range(HALO)]
        scatter(recv_far, (0, NTILE), days, lhs_ref, rhs_ref, field, 0)

    def stencil(src, at, rows):
        v = src[at + (rows,)]
        e = src[at + (slice(rows.start + 1, rows.stop + 1),)]
        w = src[at + (slice(rows.start - 1, rows.stop - 1),)]
        north = pltpu.roll(v, LAT - 1, 1)
        south = pltpu.roll(v, 1, 1)
        return (
            coef_ref[0, rows] * v
            - coef_ref[1, rows] * (e + w)
            - coef_ref[2, rows] * north
            - coef_ref[3, rows] * south
        )

    def keep(e, plane):
        hi, lo = split2(plane)
        smooth_hi[e] = hi.astype(BF16)
        smooth_lo[e] = lo.astype(BF16)

    def smooth(e):
        field[e, PAD - 2 : PAD] = edges[e, :2]
        field[e, PAD + LON_DEV : PAD + LON_DEV + 2] = edges[e, 2:]
        for rows in (
            slice(PAD, PAD + LON_DEV),
            slice(PAD - 1, PAD),
            slice(PAD + LON_DEV, PAD + LON_DEV + 1),
        ):
            once[rows] = stencil(field, (e,), rows)
        twice = stencil(once, (), slice(PAD, PAD + LON_DEV))
        keep(e, twice)
        return twice

    def mix(pair):
        window = range(2 * pair, 2 * pair + LAGS + 1)
        hi = jnp.concatenate([smooth_hi[e] for e in window], axis=1)
        lo = jnp.concatenate([smooth_lo[e] for e in window], axis=1)
        first = dot_nt(mix_ref[...], hi)
        second = dot_nt(mix_ref[: 2 * LAT], lo)
        mixed = first[: 2 * LAT] + (first[2 * LAT :] + second)
        out_ref[day_of(2 * pair)] = mixed[:LAT]
        out_ref[day_of(2 * pair + 1)] = mixed[LAT:]

    for copy in class_copies:
        copy.wait()
    coefficients(class_halo[0], slice(0, PAD))
    coefficients(class_halo[1], slice(PAD + LON_DEV, 2 * PAD + LON_DEV))
    for group in range(len(GROUPS)):
        own(group)
    near_copies = []
    for i, e in enumerate((HALO + DAY_DEV - 1, HALO + DAY_DEV - 2)):
        copy = pltpu.make_async_remote_copy(
            near_out.at[i], near_in.at[i], near_send.at[i], near_recv.at[i], device_id={"year": near}
        )
        copy.start()
        near_copies.append(copy)

    for copy in forwarded:
        copy.wait_recv()

    @section
    def _():
        scatter_far()
        for d in range(DAY_DEV - 2):
            smooth(HALO + d)
        mix(1)
        mix(2)

    for copy in near_copies + edge_copies:
        copy.wait()
    for i in range(HALO):
        keep(HALO + DAY_DEV + i, near_in[i])
    mix(3)
    smooth(1)
    smooth(0)
    mix(0)

    pltpu.make_async_remote_copy(
        recv_own.at[pl.ds(1, NTILE - 1)],
        recv_own.at[pl.ds(1, NTILE - 1)],
        list_send,
        list_recv.at[0],
        device_id={"tile": east},
    ).wait_send()
    for copy in forwarded:
        copy.wait_send()


def body(station_tile, station_cell, station_value, class_ids, coeff_table, lag_blocks):
    hbm = pl.BlockSpec(memory_space=pltpu.HBM)
    dma = pltpu.SemaphoreType.DMA
    groups = len(GROUPS)
    return pl.pallas_call(
        kernel,
        out_shape=pltpu.VMEM((DAY_DEV, LAT, LON_DEV), F32),
        in_specs=[hbm] * 6,
        out_specs=pl.BlockSpec(memory_space=pltpu.VMEM),
        scratch_shapes=[
            pltpu.VMEM((8, LANES), jnp.int32),
            pltpu.VMEM((8, LANES), jnp.int32),
            pltpu.VMEM((8, LANES), F32),
            pltpu.VMEM((LAT, LON_DEV), jnp.int32),
            pltpu.SMEM((3, NCLASS), F32),
            pltpu.VMEM((LAGS, LAT, LAT), F32),
            pltpu.VMEM((5 * NTILE, 8 * LANES), BF16),
            pltpu.VMEM((LANES, 8 * LANES), BF16),
            pltpu.VMEM((NTILE + 2, 2, LANES), F32),
            pltpu.VMEM((NTILE, 3, 2, LANES), F32),
            pltpu.VMEM((NTILE, 2, LANES), F32),
            pltpu.VMEM((LON_DEV, LAT), jnp.int32),
            pltpu.VMEM((2, PAD, LAT), jnp.int32),
            pltpu.VMEM((4, LON_DEV + 2 * PAD, LAT), F32),
            pltpu.VMEM((3 * LON_DEV, MOST * CAP), F8),
            pltpu.VMEM((DAY_DEV * LAT, MOST * CAP), F8),
            pltpu.VMEM((8 * DAY_DEV, 2 * MOST * CAP), BF16),
            pltpu.VMEM((LAT, 2 * MOST * CAP), BF16),
            pltpu.VMEM((DAYS_EXT, LON_DEV + 2 * PAD, LAT), F32),
            pltpu.VMEM((DAYS_EXT, 4, LAT), F32),
            pltpu.VMEM((LON_DEV + 2 * PAD, LAT), F32),
            pltpu.VMEM((4 * LAT, (LAGS + 1) * LAT), BF16),
            pltpu.VMEM((DAYS_EXT, LON_DEV, LAT), BF16),
            pltpu.VMEM((DAYS_EXT, LON_DEV, LAT), BF16),
            pltpu.VMEM((HALO, LON_DEV, LAT), F32),
            pltpu.VMEM((HALO, LON_DEV, LAT), F32),
            dma((6,)),
            dma,
            dma((groups,)),
            dma((groups,)),
            dma((groups,)),
            dma((HALO,)),
            dma((HALO,)),
            dma((HALO,)),
            dma((HALO,)),
            dma((2,)),
            dma((2,)),
        ],
        compiler_params=pltpu.CompilerParams(
            collective_id=0, has_side_effects=True, vmem_limit_bytes=40 * 2**20
        ),
    )(
        *(
            pltpu.with_memory_space_constraint(x, pltpu.HBM)
            for x in (
                station_tile.reshape(8, LANES),
                station_cell.reshape(8, LANES),
                station_value.reshape(8, LANES),
                class_ids,
                coeff_table,
                lag_blocks,
            )
        )
    )


def solution(mesh):
    in_specs = (
        P(("year", "tile"), None),
        P(("year", "tile")),
        P(("year", "tile")),
        P(None, "tile"),
        P(),
        P(),
    )
    out_specs = P("year", None, "tile")
    return jax.shard_map(body, mesh=mesh, in_specs=in_specs, out_specs=out_specs, check_vma=False)
```

```python
import jax
import jax.numpy as jnp
from jax import lax
from jax.experimental import pallas as pl
from jax.experimental.pallas import tpu as pltpu
from jax.sharding import PartitionSpec as P

DAY_DEV = 8
LAT = 128
LON_DEV = 256
CAP = 96
LANES = 128
NTILE = 32
NYEAR = 4
NCLASS = 16
GROUPS = ((0, 32),)
MOST = 32
LAGS = 5
HALO = 2
DAYS_EXT = DAY_DEV + 2 * HALO
PAD = 8
F32 = jnp.float32
BF16 = jnp.bfloat16
F8 = jnp.float8_e4m3fn


def dot_nt(a, b):
    return lax.dot_general(a, b, (((1,), (1,)), ((), ())), preferred_element_type=F32)


def split2(x):
    hi = x.astype(BF16).astype(F32)
    return hi, x - hi


def hot(mask):
    return jnp.where(mask, 1.0, 0.0).astype(BF16)


def hops(offset):
    return sum(min(o, n - o) * step for o, n, step in zip(offset, (4, 2, 4), (1, 2, 1)))


OFFSETS = sorted(((x, z, y) for x in range(4) for z in range(2) for y in range(4)), key=hops)


def spread(row, count):
    few = jnp.broadcast_to(row.astype(F32), (16, LANES)).astype(BF16)
    return jnp.concatenate([few] * (count // 16), axis=0)


def numbers(count):
    return lax.broadcasted_iota(jnp.int32, (count, LANES), 0).astype(F32).astype(BF16)


def pick(row, iota, piece=None):
    count = iota.shape[0]
    value = jnp.ones((), BF16) if piece is None else spread(piece, count)
    return jnp.where(spread(row, count) == iota, value, jnp.zeros((), BF16))


def bucket(tile, cell, value, pieces_ref, slots_ref, send_ref):
    hi, mid = split2(value)
    day = jnp.right_shift(cell, 15).astype(F32)
    row = jnp.bitwise_and(jnp.right_shift(cell, 8), 127).astype(F32)
    col = jnp.bitwise_and(cell, 255).astype(F32)
    of_tile = lax.broadcasted_iota(jnp.int32, (NTILE, LANES), 0)
    masks = [tile[b : b + 1, :] == of_tile for b in range(8)]
    ones = jnp.concatenate([hot(m) for m in masks], axis=0)
    source = lax.broadcasted_iota(jnp.int32, (LANES, 2 * LANES), 0)
    target = lax.broadcasted_iota(jnp.int32, (LANES, 2 * LANES), 1)
    before = hot((source < target) | (target >= LANES))
    counts = jnp.dot(ones, before, preferred_element_type=F32)
    base = jnp.zeros((NTILE, LANES), F32)
    slot_iota = lax.broadcasted_iota(jnp.int32, (LANES, LANES), 0).astype(F32)
    for b in range(8):
        lanes = slice(b * LANES, (b + 1) * LANES)
        rank = counts[b * NTILE : (b + 1) * NTILE, :LANES] + base
        base = base + counts[b * NTILE : (b + 1) * NTILE, LANES:]
        slot = jnp.sum(jnp.where(masks[b], rank, 0.0), axis=0, keepdims=True)
        slots_ref[:, lanes] = hot(slot_iota == slot)
        for q, piece in enumerate((hi, mid, day, row, col)):
            pieces_ref[q * NTILE : (q + 1) * NTILE, lanes] = jnp.where(
                masks[b], piece[b : b + 1, :], 0.0
            ).astype(BF16)
    out = dot_nt(pieces_ref[...], slots_ref[...])
    part = [out[q * NTILE : (q + 1) * NTILE] for q in range(5)]
    values = part[0] + part[1]
    cells = part[2] * 32768.0 + part[3] * 256.0 + part[4]
    for q, x in enumerate((values, cells)):
        send_ref[1 : NTILE + 1, q, :] = x
        send_ref[0:1, q, :] = x[NTILE - 1 :]
        send_ref[NTILE + 1 : NTILE + 2, q, :] = x[:1]


def dense(lists):
    lane = lax.broadcasted_iota(jnp.int32, (1, LANES), 1)
    turned = [pltpu.roll(lists, shift, 1) for shift in (96, 64, 32)]
    return [
        jnp.where(lane < CAP, lists[i + j : i + j + 1], turned[j][i + 3 : i + 4])
        for i in range(0, lists.shape[0], 4)
        for j in range(3)
    ]


def entries(recv_ref, senders, which):
    at = slice(senders[0], sum(senders))
    if len(recv_ref.shape) == 3:
        value, cell = recv_ref[at, 0, :], recv_ref[at, 1, :]
    else:
        value, cell = recv_ref[at, which, 0, :], recv_ref[at, which, 1, :]
    hi, lo = split2(value)
    return hi, lo, cell.astype(jnp.int32)


def size_of(value):
    return jnp.maximum(jnp.max(jnp.abs(value), axis=(0, 1), keepdims=True), 1e-35)


def eighths(value, largest):
    rest = value * (256.0 / largest)
    pieces = []
    for _ in range(3):
        piece = rest.astype(F8).astype(F32)
        rest = (rest - piece) * 16.0
        pieces.append(dense(piece))
    return pieces


def scatter(recv_ref, senders, days, lhs_ref, rhs_ref, field, first):
    hi, lo, cell = entries(recv_ref, senders, 1)
    largest = size_of(hi + lo)
    pieces = eighths(hi + lo, largest)
    col = dense(jnp.bitwise_and(cell, 255))
    plane = dense(jnp.right_shift(cell, 8))
    depth = len(col) * LANES
    column, latitude = numbers(LON_DEV), numbers(LAT)
    for k in range(len(col)):
        lanes = slice(k * LANES, (k + 1) * LANES)
        for q, piece in enumerate(pieces):
            lhs_ref[q * LON_DEV : (q + 1) * LON_DEV, lanes] = pick(col[k], column, piece[k]).astype(F8)
    for i, d in enumerate(days):
        for k in range(len(col)):
            rhs_ref[i * LAT : (i + 1) * LAT, k * LANES : (k + 1) * LANES] = pick(
                plane[k] - d * LAT, latitude
            ).astype(F8)
    for pair in range(len(days) // 2):
        both = dot_nt(
            lhs_ref[:, :depth], rhs_ref[2 * LAT * pair : 2 * LAT * (pair + 1), :depth]
        )
        small = both[LON_DEV : 2 * LON_DEV] + both[2 * LON_DEV :] * (1.0 / 16.0)
        both = (both[:LON_DEV] + small * (1.0 / 16.0)) * (largest * (1.0 / 256.0))
        for i in range(2):
            part = both[:, i * LAT : (i + 1) * LAT]
            e = first + 2 * pair + i
            if senders[0] == 0:
                field[e, PAD : PAD + LON_DEV] = part
            else:
                field[e, PAD : PAD + LON_DEV] += part


def scatter_edges(recv_ref, senders, count, number_of, lhs_ref, rhs_ref, edges, first):
    rows = 4 * count
    latitude, number = numbers(LAT), numbers(rows)
    blocks = 3 * senders[1] // 4
    found = [entries(recv_ref, senders, which) for which in (0, 2)]
    largest = size_of(jnp.maximum(*(jnp.abs(hi + lo) for hi, lo, _ in found)))
    for j, (hi, lo, cell) in enumerate(found):
        col = jnp.bitwise_and(cell, 255)
        near = col >= LON_DEV - 2 if j == 0 else col < 2
        place = 4 * number_of(jnp.right_shift(cell, 15)) + (
            col - (LON_DEV - 2) if j == 0 else col + 2
        )
        place = dense(jnp.where(near, place, -1))
        lat = dense(jnp.bitwise_and(jnp.right_shift(cell, 8), LAT - 1))
        pieces = eighths(hi + lo, largest)
        for k in range(blocks):
            lanes = slice((blocks * j + k) * LANES, (blocks * j + k + 1) * LANES)
            for q, piece in enumerate(pieces):
                lhs_ref[q * rows : (q + 1) * rows, lanes] = pick(
                    place[k], number, piece[k]
                ).astype(F8)
            rhs_ref[:, lanes] = pick(lat[k], latitude).astype(F8)
    depth = 2 * blocks * LANES
    both = dot_nt(lhs_ref[:, :depth], rhs_ref[:, :depth])
    small = both[rows : 2 * rows] + both[2 * rows :] * (1.0 / 16.0)
    both = (both[:rows] + small * (1.0 / 16.0)) * (largest * (1.0 / 256.0))
    for i in range(count):
        if senders[0] == 0:
            edges[first + i] = both[4 * i : 4 * i + 4]
        else:
            edges[first + i] += both[4 * i : 4 * i + 4]


def kernel(
    tile_hbm,
    cell_hbm,
    value_hbm,
    class_hbm,
    coeff_hbm,
    lag_hbm,
    out_ref,
    tile_ref,
    cell_ref,
    value_ref,
    class_ref,
    coeff_ref,
    lag_ref,
    pieces_ref,
    slots_ref,
    send_ref,
    recv_own,
    recv_far,
    class_t,
    class_halo,
    coef_ref,
    lhs_ref,
    rhs_ref,
    edge_lhs,
    edge_rhs,
    field,
    edges,
    once,
    mix_ref,
    smooth_hi,
    smooth_lo,
    near_out,
    near_in,
    load_sem,
    list_send,
    list_recv,
    far_send,
    far_recv,
    near_send,
    near_recv,
    edge_send,
    edge_recv,
    class_send,
    class_recv,
):
    loads = [
        pltpu.make_async_copy(source, target, load_sem.at[i])
        for i, (source, target) in enumerate(
            (
                (tile_hbm, tile_ref),
                (cell_hbm, cell_ref),
                (value_hbm, value_ref),
                (class_hbm, class_ref),
                (coeff_hbm, coeff_ref),
                (lag_hbm, lag_ref),
            )
        )
    ]
    for load in loads[:3]:
        load.start()

    segment = lax.axis_index("year")
    me = lax.axis_index("tile")
    odd = lax.rem(segment, 2)
    near = segment + 1 - 2 * odd
    far = lax.rem(segment + NYEAR - 1 + 2 * odd, NYEAR)

    def day_of(d):
        return d + odd * (DAY_DEV - 1 - 2 * d)

    east = lax.rem(me + 1, NTILE)
    west = lax.rem(me + NTILE - 1, NTILE)
    x, z, y = me // 8, lax.rem(me // 4, 2), lax.rem(me, 4)
    peers = [
        lax.rem(x + dx, 4) * 8 + lax.rem(z + dz, 2) * 4 + lax.rem(y + dy, 4)
        for dx, dz, dy in OFFSETS
    ]

    barrier = pltpu.get_barrier_semaphore()
    for i in reversed(range(1, NTILE)):
        pl.semaphore_signal(barrier, inc=1, device_id={"tile": peers[i]})
    pl.semaphore_signal(barrier, inc=1, device_id={"year": near})
    pl.semaphore_signal(barrier, inc=1, device_id={"year": far})
    for load in loads[3:]:
        load.start()

    for load in loads[:3]:
        load.wait()
    bucket(tile_ref[...], cell_ref[...], value_ref[...], pieces_ref, slots_ref, send_ref)

    pl.semaphore_wait(barrier, NTILE + 1)

    for g, (low, count) in reversed(list(enumerate(GROUPS))):
        for i in reversed(range(max(low, 1), low + count)):
            pltpu.make_async_remote_copy(
                send_ref.at[pl.ds(peers[i], 3)],
                recv_own.at[i],
                list_send,
                list_recv.at[g],
                device_id={"tile": peers[i]},
            ).start()
    recv_own[0] = send_ref[pl.ds(me, 3)]
    loads[3].wait()
    class_t[...] = jnp.transpose(class_ref[...])
    class_copies = [
        pltpu.make_async_remote_copy(
            class_t.at[pl.ds(start, PAD)],
            class_halo.at[1 - side],
            class_send.at[side],
            class_recv.at[1 - side],
            device_id={"tile": tgt},
        )
        for side, start, tgt in ((0, 0, west), (1, LON_DEV - PAD, east))
    ]
    for copy in class_copies:
        copy.start()

    loads[4].wait()
    loads[5].wait()
    mix_ref[...] = jnp.zeros_like(mix_ref)
    for k in range(LAGS):
        hi, lo = split2(lag_ref[k + odd * (LAGS - 1 - 2 * k)])
        for i in range(2):
            lanes = slice((k + i) * LAT, (k + i + 1) * LAT)
            mix_ref[i * LAT : (i + 1) * LAT, lanes] = hi.astype(BF16)
            mix_ref[(2 + i) * LAT : (3 + i) * LAT, lanes] = lo.astype(BF16)

    def coefficients(ids, rows):
        kappa = hzon = hmer = jnp.zeros(ids.shape, F32)
        for c in range(NCLASS):
            here = ids == c
            kappa = jnp.where(here, coeff_ref[0, c], kappa)
            hzon = jnp.where(here, coeff_ref[1, c], hzon)
            hmer = jnp.where(here, coeff_ref[2, c], hmer)
        lane = lax.broadcasted_iota(jnp.int32, ids.shape, 1)
        coef_ref[0, rows] = kappa + 2.0 * hzon + 2.0 * hmer
        coef_ref[1, rows] = hzon
        coef_ref[2, rows] = jnp.where(lane < LAT - 1, hmer, 0.0)
        coef_ref[3, rows] = jnp.where(lane > 0, hmer, 0.0)

    coefficients(class_t[...], slice(PAD, PAD + LON_DEV))

    def section(f):
        pl.when(me < NTILE)(f)

    forwarded = []
    edge_copies = [
        pltpu.make_async_remote_copy(
            edges.at[HALO + i],
            edges.at[HALO - 1 - i],
            edge_send.at[i],
            edge_recv.at[HALO - 1 - i],
            device_id={"year": far},
        )
        for i in range(HALO)
    ]

    def own(group):
        start, count = GROUPS[group]
        low = max(1, start)
        pltpu.make_async_remote_copy(
            recv_own.at[pl.ds(low, start + count - low)],
            recv_own.at[pl.ds(low, start + count - low)],
            list_send,
            list_recv.at[group],
            device_id={"tile": east},
        ).wait_recv()
        copy = pltpu.make_async_remote_copy(
            recv_own.at[pl.ds(start, count), 1],
            recv_far.at[pl.ds(start, count)],
            far_send.at[group],
            far_recv.at[group],
            device_id={"year": far},
        )
        copy.start()
        forwarded.append(copy)
        days = [day_of(d) for d in range(DAY_DEV)]

        @section
        def _():
            scatter_edges(
                recv_own, GROUPS[group], DAY_DEV, day_of, edge_lhs, edge_rhs, edges, HALO
            )

        if group == len(GROUPS) - 1:
            for copy in edge_copies:
                copy.start()

        @section
        def _():
            scatter(recv_own, GROUPS[group], days, lhs_ref, rhs_ref, field, HALO)
            if group == len(GROUPS) - 1:
                for i, e in enumerate((HALO + DAY_DEV - 1, HALO + DAY_DEV - 2)):
                    near_out[i] = smooth(e)

    def scatter_far():
        days = [day_of(d + DAY_DEV - HALO) for d in range(HALO)]
        scatter(recv_far, (0, NTILE), days, lhs_ref, rhs_ref, field, 0)

    def stencil(src, at, rows):
        v = src[at + (rows,)]
        e = src[at + (slice(rows.start + 1, rows.stop + 1),)]
        w = src[at + (slice(rows.start - 1, rows.stop - 1),)]
        north = pltpu.roll(v, LAT - 1, 1)
        south = pltpu.roll(v, 1, 1)
        return (
            coef_ref[0, rows] * v
            - coef_ref[1, rows] * (e + w)
            - coef_ref[2, rows] * north
            - coef_ref[3, rows] * south
        )

    def keep(e, plane):
        hi, lo = split2(plane)
        smooth_hi[e] = hi.astype(BF16)
        smooth_lo[e] = lo.astype(BF16)

    def smooth(e):
        field[e, PAD - 2 : PAD] = edges[e, :2]
        field[e, PAD + LON_DEV : PAD + LON_DEV + 2] = edges[e, 2:]
        for rows in (
            slice(PAD, PAD + LON_DEV),
            slice(PAD - 1, PAD),
            slice(PAD + LON_DEV, PAD + LON_DEV + 1),
        ):
            once[rows] = stencil(field, (e,), rows)
        twice = stencil(once, (), slice(PAD, PAD + LON_DEV))
        keep(e, twice)
        return twice

    def mix(pair):
        window = range(2 * pair, 2 * pair + LAGS + 1)
        hi = jnp.concatenate([smooth_hi[e] for e in window], axis=1)
        lo = jnp.concatenate([smooth_lo[e] for e in window], axis=1)
        first = dot_nt(mix_ref[...], hi)
        second = dot_nt(mix_ref[: 2 * LAT], lo)
        mixed = first[: 2 * LAT] + (first[2 * LAT :] + second)
        out_ref[day_of(2 * pair)] = mixed[:LAT]
        out_ref[day_of(2 * pair + 1)] = mixed[LAT:]

    for copy in class_copies:
        copy.wait()
    coefficients(class_halo[0], slice(0, PAD))
    coefficients(class_halo[1], slice(PAD + LON_DEV, 2 * PAD + LON_DEV))
    for group in range(len(GROUPS)):
        own(group)
    near_copies = []
    for i, e in enumerate((HALO + DAY_DEV - 1, HALO + DAY_DEV - 2)):
        copy = pltpu.make_async_remote_copy(
            near_out.at[i], near_in.at[i], near_send.at[i], near_recv.at[i], device_id={"year": near}
        )
        copy.start()
        near_copies.append(copy)

    for copy in forwarded:
        copy.wait_recv()
    for copy in edge_copies:
        copy.wait()

    @section
    def _():
        scatter_far()
        for d in range(DAY_DEV - 2):
            smooth(HALO + d)
        mix(1)
        mix(2)
        smooth(1)
        smooth(0)
        mix(0)

    for copy in near_copies:
        copy.wait()
    for i in range(HALO):
        keep(HALO + DAY_DEV + i, near_in[i])
    mix(3)

    pltpu.make_async_remote_copy(
        recv_own.at[pl.ds(1, NTILE - 1)],
        recv_own.at[pl.ds(1, NTILE - 1)],
        list_send,
        list_recv.at[0],
        device_id={"tile": east},
    ).wait_send()
    for copy in forwarded:
        copy.wait_send()


def body(station_tile, station_cell, station_value, class_ids, coeff_table, lag_blocks):
    hbm = pl.BlockSpec(memory_space=pltpu.HBM)
    dma = pltpu.SemaphoreType.DMA
    groups = len(GROUPS)
    return pl.pallas_call(
        kernel,
        out_shape=pltpu.VMEM((DAY_DEV, LAT, LON_DEV), F32),
        in_specs=[hbm] * 6,
        out_specs=pl.BlockSpec(memory_space=pltpu.VMEM),
        scratch_shapes=[
            pltpu.VMEM((8, LANES), jnp.int32),
            pltpu.VMEM((8, LANES), jnp.int32),
            pltpu.VMEM((8, LANES), F32),
            pltpu.VMEM((LAT, LON_DEV), jnp.int32),
            pltpu.SMEM((3, NCLASS), F32),
            pltpu.VMEM((LAGS, LAT, LAT), F32),
            pltpu.VMEM((5 * NTILE, 8 * LANES), BF16),
            pltpu.VMEM((LANES, 8 * LANES), BF16),
            pltpu.VMEM((NTILE + 2, 2, LANES), F32),
            pltpu.VMEM((NTILE, 3, 2, LANES), F32),
            pltpu.VMEM((NTILE, 2, LANES), F32),
            pltpu.VMEM((LON_DEV, LAT), jnp.int32),
            pltpu.VMEM((2, PAD, LAT), jnp.int32),
            pltpu.VMEM((4, LON_DEV + 2 * PAD, LAT), F32),
            pltpu.VMEM((3 * LON_DEV, MOST * CAP), F8),
            pltpu.VMEM((DAY_DEV * LAT, MOST * CAP), F8),
            pltpu.VMEM((12 * DAY_DEV, 2 * MOST * CAP), F8),
            pltpu.VMEM((LAT, 2 * MOST * CAP), F8),
            pltpu.VMEM((DAYS_EXT, LON_DEV + 2 * PAD, LAT), F32),
            pltpu.VMEM((DAYS_EXT, 4, LAT), F32),
            pltpu.VMEM((LON_DEV + 2 * PAD, LAT), F32),
            pltpu.VMEM((4 * LAT, (LAGS + 1) * LAT), BF16),
            pltpu.VMEM((DAYS_EXT, LON_DEV, LAT), BF16),
            pltpu.VMEM((DAYS_EXT, LON_DEV, LAT), BF16),
            pltpu.VMEM((HALO, LON_DEV, LAT), F32),
            pltpu.VMEM((HALO, LON_DEV, LAT), F32),
            dma((6,)),
            dma,
            dma((groups,)),
            dma((groups,)),
            dma((groups,)),
            dma((HALO,)),
            dma((HALO,)),
            dma((HALO,)),
            dma((HALO,)),
            dma((2,)),
            dma((2,)),
        ],
        compiler_params=pltpu.CompilerParams(
            collective_id=0, has_side_effects=True, vmem_limit_bytes=40 * 2**20
        ),
    )(
        *(
            pltpu.with_memory_space_constraint(x, pltpu.HBM)
            for x in (
                station_tile.reshape(8, LANES),
                station_cell.reshape(8, LANES),
                station_value.reshape(8, LANES),
                class_ids,
                coeff_table,
                lag_blocks,
            )
        )
    )


def solution(mesh):
    in_specs = (
        P(("year", "tile"), None),
        P(("year", "tile")),
        P(("year", "tile")),
        P(None, "tile"),
        P(),
        P(),
    )
    out_specs = P("year", None, "tile")
    return jax.shard_map(body, mesh=mesh, in_specs=in_specs, out_specs=out_specs, check_vma=False)
```

```python
import jax
import jax.numpy as jnp
from jax import lax
from jax.experimental import pallas as pl
from jax.experimental.pallas import tpu as pltpu
from jax.sharding import PartitionSpec as P

DAY_DEV = 8
LAT = 128
LON_DEV = 256
CAP = 96
LANES = 128
NTILE = 32
NYEAR = 4
NCLASS = 16
GROUPS = ((0, 32),)
MOST = 32
LAGS = 5
HALO = 2
DAYS_EXT = DAY_DEV + 2 * HALO
PAD = 8
F32 = jnp.float32
BF16 = jnp.bfloat16
F8 = jnp.float8_e4m3fn


def dot_nt(a, b):
    return lax.dot_general(a, b, (((1,), (1,)), ((), ())), preferred_element_type=F32)


def split2(x):
    hi = x.astype(BF16).astype(F32)
    return hi, x - hi


def hot(mask):
    return jnp.where(mask, 1.0, 0.0).astype(BF16)


def hops(offset):
    return sum(min(o, n - o) * step for o, n, step in zip(offset, (4, 2, 4), (1, 2, 1)))


OFFSETS = sorted(((x, z, y) for x in range(4) for z in range(2) for y in range(4)), key=hops)


def spread(row, count):
    few = jnp.broadcast_to(row.astype(F32), (16, LANES)).astype(BF16)
    return jnp.concatenate([few] * (count // 16), axis=0)


def numbers(count):
    return lax.broadcasted_iota(jnp.int32, (count, LANES), 0).astype(F32).astype(BF16)


def pick(row, iota, piece=None):
    count = iota.shape[0]
    value = jnp.ones((), BF16) if piece is None else spread(piece, count)
    return jnp.where(spread(row, count) == iota, value, jnp.zeros((), BF16))


def bucket(tile, cell, value, pieces_ref, slots_ref, send_ref):
    hi, mid = split2(value)
    day = jnp.right_shift(cell, 15).astype(F32)
    row = jnp.bitwise_and(jnp.right_shift(cell, 8), 127).astype(F32)
    col = jnp.bitwise_and(cell, 255).astype(F32)
    of_tile = lax.broadcasted_iota(jnp.int32, (NTILE, LANES), 0)
    masks = [tile[b : b + 1, :] == of_tile for b in range(8)]
    ones = jnp.concatenate([hot(m) for m in masks], axis=0)
    source = lax.broadcasted_iota(jnp.int32, (LANES, 2 * LANES), 0)
    target = lax.broadcasted_iota(jnp.int32, (LANES, 2 * LANES), 1)
    before = hot((source < target) | (target >= LANES))
    counts = jnp.dot(ones, before, preferred_element_type=F32)
    base = jnp.zeros((NTILE, LANES), F32)
    slot_iota = lax.broadcasted_iota(jnp.int32, (LANES, LANES), 0).astype(F32)
    for b in range(8):
        lanes = slice(b * LANES, (b + 1) * LANES)
        rank = counts[b * NTILE : (b + 1) * NTILE, :LANES] + base
        base = base + counts[b * NTILE : (b + 1) * NTILE, LANES:]
        slot = jnp.sum(jnp.where(masks[b], rank, 0.0), axis=0, keepdims=True)
        slots_ref[:, lanes] = hot(slot_iota == slot)
        for q, piece in enumerate((hi, mid, day, row, col)):
            pieces_ref[q * NTILE : (q + 1) * NTILE, lanes] = jnp.where(
                masks[b], piece[b : b + 1, :], 0.0
            ).astype(BF16)
    out = dot_nt(pieces_ref[...], slots_ref[...])
    part = [out[q * NTILE : (q + 1) * NTILE] for q in range(5)]
    values = part[0] + part[1]
    cells = part[2] * 32768.0 + part[3] * 256.0 + part[4]
    for q, x in enumerate((values, cells)):
        send_ref[1 : NTILE + 1, q, :] = x
        send_ref[0:1, q, :] = x[NTILE - 1 :]
        send_ref[NTILE + 1 : NTILE + 2, q, :] = x[:1]


def dense(lists):
    lane = lax.broadcasted_iota(jnp.int32, (1, LANES), 1)
    turned = [pltpu.roll(lists, shift, 1) for shift in (96, 64, 32)]
    return [
        jnp.where(lane < CAP, lists[i + j : i + j + 1], turned[j][i + 3 : i + 4])
        for i in range(0, lists.shape[0], 4)
        for j in range(3)
    ]


def entries(recv_ref, senders, which):
    at = slice(senders[0], sum(senders))
    if len(recv_ref.shape) == 3:
        value, cell = recv_ref[at, 0, :], recv_ref[at, 1, :]
    else:
        value, cell = recv_ref[at, which, 0, :], recv_ref[at, which, 1, :]
    hi, lo = split2(value)
    return hi, lo, cell.astype(jnp.int32)


def size_of(value):
    return jnp.maximum(jnp.max(jnp.abs(value), axis=(0, 1), keepdims=True), 1e-35)


def eighths(value, largest):
    rest = value * (256.0 / largest)
    pieces = []
    for _ in range(3):
        piece = rest.astype(F8).astype(F32)
        rest = (rest - piece) * 16.0
        pieces.append(dense(piece))
    return pieces


def scatter(recv_ref, senders, days, lhs_ref, rhs_ref, field, first):
    hi, lo, cell = entries(recv_ref, senders, 1)
    largest = size_of(hi + lo)
    pieces = eighths(hi + lo, largest)
    col = dense(jnp.bitwise_and(cell, 255))
    plane = dense(jnp.right_shift(cell, 8))
    depth = len(col) * LANES
    column, latitude = numbers(LON_DEV), numbers(LAT)
    for k in range(len(col)):
        lanes = slice(k * LANES, (k + 1) * LANES)
        for q, piece in enumerate(pieces):
            lhs_ref[q * LON_DEV : (q + 1) * LON_DEV, lanes] = pick(col[k], column, piece[k]).astype(F8)
    for i, d in enumerate(days):
        for k in range(len(col)):
            rhs_ref[i * LAT : (i + 1) * LAT, k * LANES : (k + 1) * LANES] = pick(
                plane[k] - d * LAT, latitude
            ).astype(F8)
    for pair in range(len(days) // 2):
        both = dot_nt(
            lhs_ref[:, :depth], rhs_ref[2 * LAT * pair : 2 * LAT * (pair + 1), :depth]
        )
        small = both[LON_DEV : 2 * LON_DEV] + both[2 * LON_DEV :] * (1.0 / 16.0)
        both = (both[:LON_DEV] + small * (1.0 / 16.0)) * (largest * (1.0 / 256.0))
        for i in range(2):
            part = both[:, i * LAT : (i + 1) * LAT]
            e = first + 2 * pair + i
            if senders[0] == 0:
                field[e, PAD : PAD + LON_DEV] = part
            else:
                field[e, PAD : PAD + LON_DEV] += part


def scatter_edges(recv_ref, senders, count, number_of, lhs_ref, rhs_ref, edges, first):
    rows = 4 * count
    latitude, number = numbers(LAT), numbers(rows)
    blocks = 3 * senders[1] // 4
    found = [entries(recv_ref, senders, which) for which in (0, 2)]
    largest = size_of(jnp.maximum(*(jnp.abs(hi + lo) for hi, lo, _ in found)))
    for j, (hi, lo, cell) in enumerate(found):
        col = jnp.bitwise_and(cell, 255)
        near = col >= LON_DEV - 2 if j == 0 else col < 2
        place = 4 * number_of(jnp.right_shift(cell, 15)) + (
            col - (LON_DEV - 2) if j == 0 else col + 2
        )
        place = dense(jnp.where(near, place, -1))
        lat = dense(jnp.bitwise_and(jnp.right_shift(cell, 8), LAT - 1))
        pieces = eighths(hi + lo, largest)
        for k in range(blocks):
            lanes = slice((blocks * j + k) * LANES, (blocks * j + k + 1) * LANES)
            for q, piece in enumerate(pieces):
                lhs_ref[q * rows : (q + 1) * rows, lanes] = pick(
                    place[k], number, piece[k]
                ).astype(F8)
            rhs_ref[:, lanes] = pick(lat[k], latitude).astype(F8)
    depth = 2 * blocks * LANES
    both = dot_nt(lhs_ref[:, :depth], rhs_ref[:, :depth])
    small = both[rows : 2 * rows] + both[2 * rows :] * (1.0 / 16.0)
    both = (both[:rows] + small * (1.0 / 16.0)) * (largest * (1.0 / 256.0))
    for i in range(count):
        if senders[0] == 0:
            edges[first + i] = both[4 * i : 4 * i + 4]
        else:
            edges[first + i] += both[4 * i : 4 * i + 4]


def kernel(
    tile_hbm,
    cell_hbm,
    value_hbm,
    class_hbm,
    coeff_hbm,
    lag_hbm,
    out_ref,
    mix_ref,
    smooth_hi,
    smooth_lo,
    tile_ref,
    cell_ref,
    value_ref,
    class_ref,
    coeff_ref,
    lag_ref,
    pieces_ref,
    slots_ref,
    send_ref,
    recv_own,
    recv_far,
    class_t,
    class_halo,
    coef_ref,
    lhs_ref,
    rhs_ref,
    edge_lhs,
    edge_rhs,
    field,
    edges,
    once,
    near_out,
    near_in,
    load_sem,
    list_send,
    list_recv,
    far_send,
    far_recv,
    near_send,
    near_recv,
    edge_send,
    edge_recv,
    class_send,
    class_recv,
):
    loads = [
        pltpu.make_async_copy(source, target, load_sem.at[i])
        for i, (source, target) in enumerate(
            (
                (tile_hbm, tile_ref),
                (cell_hbm, cell_ref),
                (value_hbm, value_ref),
                (class_hbm, class_ref),
                (coeff_hbm, coeff_ref),
                (lag_hbm, lag_ref),
            )
        )
    ]
    for load in loads[:3]:
        load.start()

    segment = lax.axis_index("year")
    me = lax.axis_index("tile")
    odd = lax.rem(segment, 2)
    near = segment + 1 - 2 * odd
    far = lax.rem(segment + NYEAR - 1 + 2 * odd, NYEAR)

    def day_of(d):
        return d + odd * (DAY_DEV - 1 - 2 * d)

    east = lax.rem(me + 1, NTILE)
    west = lax.rem(me + NTILE - 1, NTILE)
    x, z, y = me // 8, lax.rem(me // 4, 2), lax.rem(me, 4)
    peers = [
        lax.rem(x + dx, 4) * 8 + lax.rem(z + dz, 2) * 4 + lax.rem(y + dy, 4)
        for dx, dz, dy in OFFSETS
    ]

    barrier = pltpu.get_barrier_semaphore()
    for i in reversed(range(1, NTILE)):
        pl.semaphore_signal(barrier, inc=1, device_id={"tile": peers[i]})
    pl.semaphore_signal(barrier, inc=1, device_id={"year": near})
    pl.semaphore_signal(barrier, inc=1, device_id={"year": far})
    for load in loads[3:]:
        load.start()

    for load in loads[:3]:
        load.wait()
    bucket(tile_ref[...], cell_ref[...], value_ref[...], pieces_ref, slots_ref, send_ref)

    pl.semaphore_wait(barrier, NTILE + 1)

    for g, (low, count) in reversed(list(enumerate(GROUPS))):
        for i in reversed(range(max(low, 1), low + count)):
            pltpu.make_async_remote_copy(
                send_ref.at[pl.ds(peers[i], 3)],
                recv_own.at[i],
                list_send,
                list_recv.at[g],
                device_id={"tile": peers[i]},
            ).start()
    recv_own[0] = send_ref[pl.ds(me, 3)]
    loads[3].wait()
    class_t[...] = jnp.transpose(class_ref[...])
    class_copies = [
        pltpu.make_async_remote_copy(
            class_t.at[pl.ds(start, PAD)],
            class_halo.at[1 - side],
            class_send.at[side],
            class_recv.at[1 - side],
            device_id={"tile": tgt},
        )
        for side, start, tgt in ((0, 0, west), (1, LON_DEV - PAD, east))
    ]
    for copy in class_copies:
        copy.start()

    loads[4].wait()
    loads[5].wait()
    mix_ref[...] = jnp.zeros_like(mix_ref)
    for k in range(LAGS):
        hi, lo = split2(lag_ref[k + odd * (LAGS - 1 - 2 * k)])
        for i in range(2):
            lanes = slice((k + i) * LAT, (k + i + 1) * LAT)
            mix_ref[i * LAT : (i + 1) * LAT, lanes] = hi.astype(BF16)
            mix_ref[(2 + i) * LAT : (3 + i) * LAT, lanes] = lo.astype(BF16)

    def coefficients(ids, rows):
        kappa = hzon = hmer = jnp.zeros(ids.shape, F32)
        for c in range(NCLASS):
            here = ids == c
            kappa = jnp.where(here, coeff_ref[0, c], kappa)
            hzon = jnp.where(here, coeff_ref[1, c], hzon)
            hmer = jnp.where(here, coeff_ref[2, c], hmer)
        lane = lax.broadcasted_iota(jnp.int32, ids.shape, 1)
        coef_ref[0, rows] = kappa + 2.0 * hzon + 2.0 * hmer
        coef_ref[1, rows] = hzon
        coef_ref[2, rows] = jnp.where(lane < LAT - 1, hmer, 0.0)
        coef_ref[3, rows] = jnp.where(lane > 0, hmer, 0.0)

    coefficients(class_t[...], slice(PAD, PAD + LON_DEV))

    def section(f):
        pl.when(me < NTILE)(f)

    forwarded = []
    edge_copies = [
        pltpu.make_async_remote_copy(
            edges.at[HALO + i],
            edges.at[HALO - 1 - i],
            edge_send.at[i],
            edge_recv.at[HALO - 1 - i],
            device_id={"year": far},
        )
        for i in range(HALO)
    ]

    def own(group):
        start, count = GROUPS[group]
        low = max(1, start)
        pltpu.make_async_remote_copy(
            recv_own.at[pl.ds(low, start + count - low)],
            recv_own.at[pl.ds(low, start + count - low)],
            list_send,
            list_recv.at[group],
            device_id={"tile": east},
        ).wait_recv()
        copy = pltpu.make_async_remote_copy(
            recv_own.at[pl.ds(start, count), 1],
            recv_far.at[pl.ds(start, count)],
            far_send.at[group],
            far_recv.at[group],
            device_id={"year": far},
        )
        copy.start()
        forwarded.append(copy)
        days = [day_of(d) for d in range(DAY_DEV)]

        @section
        def _():
            scatter_edges(
                recv_own, GROUPS[group], DAY_DEV, day_of, edge_lhs, edge_rhs, edges, HALO
            )

        if group == len(GROUPS) - 1:
            for copy in edge_copies:
                copy.start()

        @section
        def _():
            scatter(recv_own, GROUPS[group], days, lhs_ref, rhs_ref, field, HALO)
            if group == len(GROUPS) - 1:
                for i, e in enumerate((HALO + DAY_DEV - 1, HALO + DAY_DEV - 2)):
                    near_out[i] = smooth(e)

    def scatter_far():
        days = [day_of(d + DAY_DEV - HALO) for d in range(HALO)]
        scatter(recv_far, (0, NTILE), days, lhs_ref, rhs_ref, field, 0)

    def stencil(src, at, rows):
        v = src[at + (rows,)]
        e = src[at + (slice(rows.start + 1, rows.stop + 1),)]
        w = src[at + (slice(rows.start - 1, rows.stop - 1),)]
        north = pltpu.roll(v, LAT - 1, 1)
        south = pltpu.roll(v, 1, 1)
        return (
            coef_ref[0, rows] * v
            - coef_ref[1, rows] * (e + w)
            - coef_ref[2, rows] * north
            - coef_ref[3, rows] * south
        )

    def keep(e, plane):
        hi, lo = split2(plane)
        smooth_hi[e] = hi.astype(BF16)
        smooth_lo[e] = lo.astype(BF16)

    def smooth(e):
        field[e, PAD - 2 : PAD] = edges[e, :2]
        field[e, PAD + LON_DEV : PAD + LON_DEV + 2] = edges[e, 2:]
        for rows in (
            slice(PAD, PAD + LON_DEV),
            slice(PAD - 1, PAD),
            slice(PAD + LON_DEV, PAD + LON_DEV + 1),
        ):
            once[rows] = stencil(field, (e,), rows)
        twice = stencil(once, (), slice(PAD, PAD + LON_DEV))
        keep(e, twice)
        return twice

    def mix(pair):
        mixed = mix_days(pair, mix_ref, smooth_hi, smooth_lo)
        out_ref[2 * pair] = mixed[:LAT]
        out_ref[2 * pair + 1] = mixed[LAT:]

    for copy in class_copies:
        copy.wait()
    coefficients(class_halo[0], slice(0, PAD))
    coefficients(class_halo[1], slice(PAD + LON_DEV, 2 * PAD + LON_DEV))
    for group in range(len(GROUPS)):
        own(group)
    near_copies = []
    for i, e in enumerate((HALO + DAY_DEV - 1, HALO + DAY_DEV - 2)):
        copy = pltpu.make_async_remote_copy(
            near_out.at[i], near_in.at[i], near_send.at[i], near_recv.at[i], device_id={"year": near}
        )
        copy.start()
        near_copies.append(copy)

    for copy in forwarded:
        copy.wait_recv()
    for copy in edge_copies:
        copy.wait()

    @section
    def _():
        scatter_far()
        for d in range(DAY_DEV - 2):
            smooth(HALO + d)
        mix(1)
        mix(2)
        smooth(1)
        smooth(0)
        mix(0)

    for copy in near_copies:
        copy.wait()
    for i in range(HALO):
        keep(HALO + DAY_DEV + i, near_in[i])

    pltpu.make_async_remote_copy(
        recv_own.at[pl.ds(1, NTILE - 1)],
        recv_own.at[pl.ds(1, NTILE - 1)],
        list_send,
        list_recv.at[0],
        device_id={"tile": east},
    ).wait_send()
    for copy in forwarded:
        copy.wait_send()


def mix_days(pair, mix_ref, smooth_hi, smooth_lo):
    window = range(2 * pair, 2 * pair + LAGS + 1)
    hi = jnp.concatenate([smooth_hi[e] for e in window], axis=1)
    lo = jnp.concatenate([smooth_lo[e] for e in window], axis=1)
    first = dot_nt(mix_ref[...], hi)
    second = dot_nt(mix_ref[: 2 * LAT], lo)
    return first[: 2 * LAT] + (first[2 * LAT :] + second)


def write_out(days_ref, mix_ref, smooth_hi, smooth_lo, out_ref, last, sems):
    odd = lax.rem(lax.axis_index("year"), 2)

    def to_day(source, d):
        copy = pltpu.make_async_copy(
            source, out_ref.at[d + odd * (DAY_DEV - 1 - 2 * d)], sems.at[d]
        )
        copy.start()
        return copy

    copies = [to_day(days_ref.at[d], d) for d in range(DAY_DEV - 2)]
    mixed = mix_days(DAY_DEV // 2 - 1, mix_ref, smooth_hi, smooth_lo)
    for i in range(2):
        last[i] = mixed[i * LAT : (i + 1) * LAT]
    copies += [to_day(last.at[i], DAY_DEV - 2 + i) for i in range(2)]
    for copy in copies:
        copy.wait()


def body(station_tile, station_cell, station_value, class_ids, coeff_table, lag_blocks):
    hbm = pl.BlockSpec(memory_space=pltpu.HBM)
    dma = pltpu.SemaphoreType.DMA
    groups = len(GROUPS)
    parts = pl.pallas_call(
        kernel,
        out_shape=[
            pltpu.VMEM((DAY_DEV - 2, LAT, LON_DEV), F32),
            pltpu.VMEM((4 * LAT, (LAGS + 1) * LAT), BF16),
            pltpu.VMEM((DAYS_EXT, LON_DEV, LAT), BF16),
            pltpu.VMEM((DAYS_EXT, LON_DEV, LAT), BF16),
        ],
        in_specs=[hbm] * 6,
        out_specs=[pl.BlockSpec(memory_space=pltpu.VMEM)] * 4,
        scratch_shapes=[
            pltpu.VMEM((8, LANES), jnp.int32),
            pltpu.VMEM((8, LANES), jnp.int32),
            pltpu.VMEM((8, LANES), F32),
            pltpu.VMEM((LAT, LON_DEV), jnp.int32),
            pltpu.SMEM((3, NCLASS), F32),
            pltpu.VMEM((LAGS, LAT, LAT), F32),
            pltpu.VMEM((5 * NTILE, 8 * LANES), BF16),
            pltpu.VMEM((LANES, 8 * LANES), BF16),
            pltpu.VMEM((NTILE + 2, 2, LANES), F32),
            pltpu.VMEM((NTILE, 3, 2, LANES), F32),
            pltpu.VMEM((NTILE, 2, LANES), F32),
            pltpu.VMEM((LON_DEV, LAT), jnp.int32),
            pltpu.VMEM((2, PAD, LAT), jnp.int32),
            pltpu.VMEM((4, LON_DEV + 2 * PAD, LAT), F32),
            pltpu.VMEM((3 * LON_DEV, MOST * CAP), F8),
            pltpu.VMEM((DAY_DEV * LAT, MOST * CAP), F8),
            pltpu.VMEM((12 * DAY_DEV, 2 * MOST * CAP), F8),
            pltpu.VMEM((LAT, 2 * MOST * CAP), F8),
            pltpu.VMEM((DAYS_EXT, LON_DEV + 2 * PAD, LAT), F32),
            pltpu.VMEM((DAYS_EXT, 4, LAT), F32),
            pltpu.VMEM((LON_DEV + 2 * PAD, LAT), F32),
            pltpu.VMEM((HALO, LON_DEV, LAT), F32),
            pltpu.VMEM((HALO, LON_DEV, LAT), F32),
            dma((6,)),
            dma,
            dma((groups,)),
            dma((groups,)),
            dma((groups,)),
            dma((HALO,)),
            dma((HALO,)),
            dma((HALO,)),
            dma((HALO,)),
            dma((2,)),
            dma((2,)),
        ],
        compiler_params=pltpu.CompilerParams(
            collective_id=0, has_side_effects=True, vmem_limit_bytes=40 * 2**20
        ),
    )(
        *(
            pltpu.with_memory_space_constraint(x, pltpu.HBM)
            for x in (
                station_tile.reshape(8, LANES),
                station_cell.reshape(8, LANES),
                station_value.reshape(8, LANES),
                class_ids,
                coeff_table,
                lag_blocks,
            )
        )
    )
    return pl.pallas_call(
        write_out,
        out_shape=jax.ShapeDtypeStruct((DAY_DEV, LAT, LON_DEV), F32),
        in_specs=[pl.BlockSpec(memory_space=pltpu.VMEM)] * 4,
        out_specs=pl.BlockSpec(memory_space=pl.ANY),
        scratch_shapes=[pltpu.VMEM((2, LAT, LON_DEV), F32), dma((DAY_DEV,))],
    )(*(pltpu.with_memory_space_constraint(x, pltpu.VMEM) for x in parts))


def solution(mesh):
    in_specs = (
        P(("year", "tile"), None),
        P(("year", "tile")),
        P(("year", "tile")),
        P(None, "tile"),
        P(),
        P(),
    )
    out_specs = P("year", None, "tile")
    return jax.shard_map(body, mesh=mesh, in_specs=in_specs, out_specs=out_specs, check_vma=False)
```
